32 devices in a mesh: lon: 8 (over z, x), lat: 4 (over y, core).
Axes of the slice: x: 2, y: 2, z: 4, core: 2. Of those that a mesh axis runs over, the one named last changes fastest.
Arguments:
- fields: float32 [5, 4, 128, 1024], P(None, None, 'lat', 'lon'), may hold values from -6 to 6
- depth: int32 [128], P('lat'), may hold values from 0 to 96, as said below
- frac: float32 [4, 128, 1024], P(None, 'lat', 'lon'), may hold values from 0 to 1
- helm: float32 [4, 128, 1024], P(None, 'lat', 'lon'), may hold values from 0.1 to 2
Outputs:
- departed: float32 [5, 4, 128, 1024], P(None, None, 'lat', 'lon')
- pressure: float32 [4, 128, 1024], P(None, 'lat', 'lon')
The draws below stay inside these ranges and needn't reach their ends.
Inputs may be any that keep to these rules, and one draw needn't show every extreme that they name: All rows of an aligned band of 8 latitude rows share one depth. A band's depth is either 96 (a jet band) or at most 32, and may be 0. Among the 32 rows of one device (aligned blocks) at most 1 band is a jet band, and in every draw some block has exactly 1.
All inputs are finite; a program needn't handle non-finite values.
Results may differ from the reference program's by a relative error of at most 0.0003.
Values sent between devices are 32-bit elements; how exact they have to be, the bound alone decides.
A program may use at most 128 MiB of HBM per device.

```python
import math
import jax
import jax.numpy as jnp

CLAT = 32
LEV = 4
BAND = 8
MAXD = 96
SHALLOW = 32
JETS = 1
NLON = 1024
NLAT = 128


def draw_depth(key, part):
    nbands = NLAT // BAND
    per_block = CLAT // BAND
    blocks = NLAT // CLAT
    key_base, key_count, key_order, key_top = jax.random.split(key, 4)
    base = jax.random.randint(key_base, (nbands,), 0, SHALLOW + 1)
    count = jax.random.randint(key_count, (blocks,), 0, JETS + 1)
    top = jax.random.randint(key_top, (), 0, blocks)
    is_top = jnp.arange(blocks) == top
    count = jnp.where(is_top, JETS, jnp.minimum(count, per_block - 1))
    order = jax.vmap(lambda k: jax.random.permutation(k, per_block))(jax.random.split(key_order, blocks))
    jet = (order < count[:, None]).reshape(nbands)
    still = ((order == per_block - 1) & jnp.logical_not(is_top)[:, None]).reshape(nbands)
    bands = jnp.where(jet, MAXD, jnp.where(still, 0, base))
    return jnp.repeat(bands, BAND).astype(jnp.int32)


def block_scale(rng, shape, cuts, low, top_value):
    gain = 1.0
    for axis_at, shards_of in cuts:
        steps = jax.random.uniform(jax.random.fold_in(jax.random.fold_in(rng, 6), axis_at), (shards_of,), jnp.float32, low / len(cuts), top_value / len(cuts))
        gain = gain * jnp.repeat(jnp.exp(steps), shape[axis_at] // shards_of).reshape((-1,) + (1,) * (len(shape) - 1 - axis_at))
    return gain


def bell_draw(own_key, dims, width, limit, cuts=(), held_as=jnp.bfloat16):
    array = jax.random.normal(own_key, dims, jnp.float32) * width
    if len(cuts) > 0:
        array = block_scale(own_key, dims, cuts, -0.22, 0.18) * array
    return jnp.clip(array, min=-limit, max=limit).astype(held_as)


def setup_inputs(seed: int = 0) -> dict:
    splits = jax.random.split(jax.random.key(seed), 5)
    return {
        "fields": bell_draw(splits[0], (5, LEV, NLAT, NLON), 1.0, 6.0, ((2, 4), (3, 8)), jnp.float32),
        "depth": draw_depth(jax.random.fold_in(splits[4], 71), 0),
        "frac": jnp.clip(1.0 * jax.random.uniform(splits[2], (LEV, NLAT, NLON), jnp.float32) ** block_scale(splits[2], (LEV, NLAT, NLON), ((1, 4), (2, 8)), -0.2, 0.2), 0.0, 1.0),
        "helm": jnp.clip(jnp.exp(math.log(2.0) - 2.9957323 * jax.random.uniform(splits[3], (LEV, NLAT, NLON), jnp.float32) ** block_scale(splits[3], (LEV, NLAT, NLON), ((1, 4), (2, 8)), -0.2, 0.2)), 0.1, 2.0),
    }


def interp_weights(frac):
    s = -frac
    return [s * (s + 1.0) * (s + 2.0) / 6.0, -(s - 1.0) * (s + 1.0) * (s + 2.0) / 2.0, (s - 1.0) * s * (s + 2.0) / 2.0, -(s - 1.0) * s * (s + 1.0) / 6.0]


def lat_next(field):
    zero_row = jnp.zeros_like(field[:, :1, :])
    return jnp.concatenate([field[:, 1:, :], zero_row], axis=1)


def lat_prev(field):
    zero_row = jnp.zeros_like(field[:, :1, :])
    return jnp.concatenate([zero_row, field[:, :-1, :]], axis=1)


def reference(fields, depth, frac, helm):
    nlon = fields.shape[3]
    column = jnp.arange(nlon, dtype=jnp.int32)
    weights = interp_weights(frac)
    offsets = [-1, 0, 1, 2]
    results = []
    for which in range(5):
        field = fields[which]
        total = jnp.zeros_like(field)
        for offset, weight in zip(offsets, weights):
            index = jnp.mod(column[None, :] - depth[:, None].astype(jnp.int32) - offset, nlon).astype(jnp.int32)
            index = jnp.broadcast_to(index[None], field.shape)
            total = total + weight * jnp.take_along_axis(field, index, axis=2)
        results.append(total)
    departed = jnp.stack(results)
    u_wind, v_wind, phi = departed[0], departed[1], departed[3]
    div = 0.5 * (jnp.roll(u_wind, -1, axis=2) - jnp.roll(u_wind, 1, axis=2) + lat_next(v_wind) - lat_prev(v_wind))
    rhs = phi - 0.5 * div
    pressure = phi
    for sweep in range(2):
        beside_all = jnp.roll(pressure, -1, axis=2) + jnp.roll(pressure, 1, axis=2) + lat_next(pressure) + lat_prev(pressure)
        pressure = (rhs + beside_all) / (4.0 + helm)
    return departed, pressure
```

```python
import functools

import jax
import jax.numpy as jnp
from jax import lax
from jax.experimental import pallas as pl
from jax.experimental.pallas import tpu as pltpu
from jax.sharding import PartitionSpec as P

BAND = 8
SHALLOW = 32
LANES = 128
NEAR = SHALLOW + 4
F32 = jnp.float32
MESH = pl.DeviceIdType.MESH
HALO_FIELDS = (0, 1, 3)
SPARE = 108


def turn(x, shift):
    shift %= LANES
    return x if shift == 0 else pltpu.roll(x, shift, axis=1)


def lane_of(shape):
    return lax.broadcasted_iota(jnp.int32, shape, len(shape) - 1)


def jet_band(depth_ref, bands):
    jet = jnp.int32(0)
    for b in range(1, bands):
        jet = jnp.where(depth_ref[b * BAND] > SHALLOW, b, jet)
    return jet


def interp_weights(frac):
    s = -frac
    below, above = (s - 1.0) * s, (s + 1.0) * (s + 2.0)
    return [
        s * above * (1.0 / 6.0),
        (s - 1.0) * above * -0.5,
        below * (s + 2.0) * 0.5,
        below * (s + 1.0) * (-1.0 / 6.0),
    ]


def depart(own, left, right, depth, weights):
    lane = lane_of(own[0].shape)
    totals = [jnp.zeros_like(own[0]) for _ in own]
    for o, w in zip((-1, 0, 1, 2), weights):
        s = depth + o
        t = lane + s
        shift = (s + LANES) & (LANES - 1)
        for n in range(len(own)):
            x = jnp.where(t <= LANES - 1, own[n], left[n])
            if o == -1:
                x = jnp.where(t == -1, right[n], x)
            totals[n] = totals[n] + w * pltpu.roll(x, shift, axis=1)
    return totals


def depart_beside(own, left, right, depth, weights):
    lane = lane_of(own[0].shape)
    totals = [jnp.zeros_like(own[0]) for _ in own]
    for o, w in zip((-1, 0, 1, 2), weights):
        s = depth + o
        t = lane + s
        shift = (s + LANES) & (LANES - 1)
        for n in range(len(own)):
            x = jnp.where(t <= LANES - 1, left[n], own[n])
            if o < 2:
                x = jnp.where((t >= 0) & (t <= 1), right[n], x)
            if o == -1:
                x = jnp.where(t == -1, own[n], x)
            totals[n] = totals[n] + w * pltpu.roll(x, shift, axis=1)
    return totals


def beside_pair(own, halo):
    lane = lane_of(own.shape)
    first, last = lane == 0, lane == LANES - 1
    return (
        (turn(jnp.where(first, halo, own), -1), turn(jnp.where(last, halo, own), 1)),
        (turn(jnp.where(first, own, halo), -1), turn(jnp.where(last, own, halo), 1)),
    )


ORDER = (0, 1, 3, 2, 4)


def whole_step(lev, clat, depth_hbm, fields_hbm, frac_hbm, helm_hbm, departed, pressure,
               depth_ref, fields, frac, helm, main, edge, top, bottom, dtop, dbottom, gtop, gbottom,
               main_i, edge_i, above, below, la, lb, ra, rb,
               ext, hel, rhs_s, p1_s, wts, in_sem, send_sem, recv_sem):
    bands = clat // BAND
    loads = [
        pltpu.make_async_copy(src, dst, in_sem.at[i])
        for i, (src, dst) in enumerate(
            ((depth_hbm, depth_ref), (fields_hbm, fields), (frac_hbm, frac), (helm_hbm, helm)))
    ]
    for load in loads:
        load.start()
    nlon, nlat = lax.axis_size("lon"), lax.axis_size("lat")
    i, j = lax.axis_index("lon"), lax.axis_index("lat")
    east, west = lax.rem(i + 1, nlon), lax.rem(i + nlon - 1, nlon)
    south, north = lax.rem(j + 1, nlat), lax.rem(j + nlat - 1, nlat)
    peers = [{"lon": a, "lat": b} for a, b in (
        (east, j), (west, j), (i, north), (i, south),
        (east, north), (east, south), (west, north), (west, south))]
    barrier = pltpu.get_barrier_semaphore()
    for peer in peers:
        pl.semaphore_signal(barrier, inc=1, device_id=peer, device_id_type=MESH)

    def copy(n, src, dst, peer):
        return pltpu.make_async_remote_copy(
            src_ref=src, dst_ref=dst, send_sem=send_sem.at[n], recv_sem=recv_sem.at[n],
            device_id=peers[peer], device_id_type=MESH)

    mains = {f: copy(7 + f, main.at[f], main_i.at[f], 0) for f in range(5)}
    west_copy = copy(0, edge, edge_i, 1)
    beyond = [
        copy(1, top, below, 2),
        copy(2, bottom, above, 3),
        copy(3, dtop, lb, 4),
        copy(4, dbottom, la, 5),
        copy(5, gtop, rb, 6),
        copy(6, gbottom, ra, 7),
    ]
    for load in loads:
        load.wait()
    jet = jet_band(depth_ref, bands)
    nk = lev * BAND
    lane = lane_of((nk, LANES))
    jets = jnp.full((nk, LANES), jet)
    rest = None
    for b in range(bands):
        at = SPARE + 3 * b
        rows = pl.ds(b * BAND, BAND)
        fr = turn(frac[:, rows, :].reshape(nk, LANES), at - (LANES - 2))
        he = turn(helm[:, rows, :].reshape(nk, LANES), at + 2 - (LANES - 1))
        rest = fr if rest is None else jnp.where(lane >= at, fr, rest)
        rest = jnp.where(lane >= at + 2, he, rest)
    for f in ORDER:
        x = [fields[f, :, pl.ds(b * BAND, BAND), :].reshape(nk, LANES) for b in range(bands)]
        deep = x[0]
        for b in range(1, bands):
            deep = jnp.where(jets == b, x[b], deep)
        packed = None
        for slot in range(bands - 1):
            y = jnp.where(jets > slot, x[slot], x[slot + 1])
            y = turn(y, slot * NEAR + NEAR - LANES)
            packed = y if packed is None else jnp.where(lane >= slot * NEAR, y, packed)
        if f == 0:
            packed = jnp.where(lane >= SPARE, rest, packed)
        main[f, 0] = deep.reshape(lev, BAND, LANES)
        main[f, 1] = packed.reshape(lev, BAND, LANES)
        if f == ORDER[0]:
            pl.semaphore_wait(barrier, len(peers))
        if f == ORDER[3]:
            acc = jnp.zeros((nk, LANES), F32)
            for b in range(bands):
                rows = pl.ds(b * BAND, BAND)
                for n in range(7):
                    src = fields[n, :, rows, :] if n < 5 else (frac if n == 5 else helm)[:, rows, :]
                    at = 32 * b + (17 if n == 6 else 3 * n)
                    wide = 3 if n < 5 else 7 - n
                    acc = jnp.where((lane >= at) & (lane < at + wide), turn(src.reshape(nk, LANES), at), acc)
            edge[...] = acc.reshape(lev, BAND, LANES)
            west_copy.start()
            lane8 = lane_of((2 * lev, LANES))
            for row, mine, diag, thin, n, at_depth in (
                    (0, top, dtop, gtop, 0, 0), (clat - 2, bottom, dbottom, gbottom, 1, clat - 1)):
                for q in range(5):
                    src = fields.at[HALO_FIELDS[q]] if q < 3 else (frac if q == 3 else helm)
                    for k in range(lev):
                        mine[q, 2 * k:2 * k + 2, :] = src[k, row:row + 2, :]
                mine[5] = jnp.full((2 * lev, LANES), depth_ref[at_depth].astype(F32))
                beyond[n].start()
                u = jnp.where(lane8 < 2, turn(mine[3], 2), mine[0])
                diag[0] = jnp.where(lane8 == 2, turn(mine[4], 3), u)
                diag[1] = mine[1]
                diag[2] = mine[2]
                beyond[2 + n].start()
                g = mine[0]
                for q in range(1, 5):
                    at = 11 if q == 4 else 3 * q
                    g = jnp.where(lane8 >= at, turn(mine[q], at), g)
                thin[...] = g
                beyond[4 + n].start()
        mains[f].start()

    for k in range(lev):
        for o, w in enumerate(interp_weights(frac[k])):
            wts[o, k] = w
        hel[0, k, pl.ds(BAND, clat), :] = helm[k]
    inside = (j > 0, j < nlat - 1)
    flat = lambda x: x.reshape(nk, LANES)
    tall3 = lambda x: x.reshape(lev, BAND, LANES)
    west_copy.wait_recv()
    for f in ORDER:
        mains[f].wait_recv()
        for b in range(bands):
            rows = pl.ds(b * BAND, BAND)
            depth = depth_ref[b * BAND]
            slot = b - (b > jet).astype(jnp.int32)
            amount = (2 * LANES - NEAR - NEAR * slot) & (LANES - 1)
            own = flat(fields[f, :, rows, :])
            left = jnp.where(jets == b, flat(main_i[f, 0]), pltpu.roll(flat(main_i[f, 1]), amount, axis=1))
            brim = flat(edge_i[...])
            right = turn(brim, -(32 * b + 3 * f))
            [got] = depart([own], [left], [right], depth, [flat(wts[o, :, rows, :]) for o in range(4)])
            departed[f, :, rows, :] = tall3(got)
            if f in HALO_FIELDS:
                q = HALO_FIELDS.index(f)
                rest = flat(main_i[0, 1])
                fr = jnp.where(lane < 64, turn(brim, -(32 * b + 15)), turn(rest, 18 - 3 * b))
                [past] = depart_beside([own], [left], [right], depth, interp_weights(fr))
                at = pl.ds((b + 1) * BAND, BAND)
                ext[q, 0, :, at, :] = tall3(got)
                ext[q, 1, :, at, :] = tall3(past)
                if f == 0:
                    he = jnp.where(lane < 64, turn(brim, -(32 * b + 17)), turn(rest, 17 - 3 * b))
                    hel[1, :, at, :] = tall3(he)
        if f == ORDER[2]:
            for c in beyond:
                c.wait_recv()
            solve(lev, clat, inside, helm, above, below, la, lb, ra, rb, ext, hel, rhs_s, p1_s, pressure)
    for c in (west_copy, *beyond, *mains.values()):
        c.wait_send()


def solve(lev, clat, inside, helm, above, below, la, lb, ra, rb, ext, hel, rhs_s, p1_s, pressure):
    lane = lane_of((BAND, LANES))
    for side, (mine, diag, thin) in enumerate(((above, la, ra), (below, lb, rb))):
        depth = jnp.max(mine[5]).astype(jnp.int32)
        own = [mine[q] for q in range(3)]
        left = [diag[q] for q in range(3)]
        g = thin[...]
        right = [turn(g, -3 * q) for q in range(3)]
        fr = jnp.where(lane < 64, turn(g, -9), turn(left[0], -2))
        he = jnp.where(lane < 64, turn(g, -11), turn(left[0], -3))
        got = depart(own, left, right, depth, interp_weights(mine[3]))
        past = depart_beside(own, left, right, depth, interp_weights(fr))
        at = BAND - 2 if side == 0 else BAND + clat
        for k in range(lev):
            pair = slice(2 * k, 2 * k + 2)
            for q in range(3):
                ext[q, 0, k, at:at + 2, :] = jnp.where(inside[side], got[q], 0.0)[pair]
                ext[q, 1, k, at:at + 2, :] = jnp.where(inside[side], past[q], 0.0)[pair]
            hel[0, k, at:at + 2, :] = mine[4][pair]
            hel[1, k, at:at + 2, :] = he[pair]
    tall = clat + BAND
    row = lax.broadcasted_iota(jnp.int32, (lev, tall, LANES), 1)
    outside = ((row == 0) & jnp.logical_not(inside[0])) | ((row == clat + 1) & jnp.logical_not(inside[1]))
    first = BAND - 1
    flat = lambda x: x.reshape(-1, LANES)
    mid, up, down = pl.ds(first, tall), pl.ds(first - 1, tall), pl.ds(first + 1, tall)
    u_all = beside_pair(flat(ext[0, 0, :, mid, :]), flat(ext[0, 1, :, mid, :]))
    phi = [flat(ext[2, h, :, mid, :]) for h in range(2)]
    phi_all = beside_pair(*phi)
    for h in range(2):
        div = 0.5 * (u_all[h][0] - u_all[h][1] + flat(ext[1, h, :, down, :]) - flat(ext[1, h, :, up, :]))
        rhs = phi[h] - 0.5 * div
        around = phi_all[h][0] + phi_all[h][1] + flat(ext[2, h, :, down, :]) + flat(ext[2, h, :, up, :])
        p1 = (rhs + around) / (4.0 + flat(hel[h, :, mid, :]))
        p1_s[h] = jnp.where(outside, 0.0, p1.reshape(lev, tall, LANES))
        if h == 0:
            rhs_s[...] = rhs.reshape(lev, tall, LANES)
    mid = pl.ds(1, clat)
    east, west = beside_pair(flat(p1_s[0, :, mid, :]), flat(p1_s[1, :, mid, :]))[0]
    around = east + west + flat(p1_s[0, :, pl.ds(2, clat), :]) + flat(p1_s[0, :, pl.ds(0, clat), :])
    pressure[...] = ((flat(rhs_s[:, mid, :]) + around) / (4.0 + flat(helm[...]))).reshape(lev, clat, LANES)


def store(departed, pressure, departed_o, pressure_o, sem):
    copies = [pltpu.make_async_copy(departed, departed_o, sem.at[0]), pltpu.make_async_copy(pressure, pressure_o, sem.at[1])]
    for c in copies:
        c.start()
    for c in copies:
        c.wait()


def local(fields, depth, frac, helm):
    lev, clat, clon = fields.shape[1:]
    hbm = pl.BlockSpec(memory_space=pltpu.HBM)
    vmem = pl.BlockSpec(memory_space=pltpu.VMEM)
    sent = [(5, 2, lev, BAND, clon), (lev, BAND, clon), (6, 2 * lev, clon), (6, 2 * lev, clon),
            (3, 2 * lev, clon), (3, 2 * lev, clon), (2 * lev, clon), (2 * lev, clon)]
    tall = clat + 2 * BAND
    departed, pressure = pl.pallas_call(
        functools.partial(whole_step, lev, clat),
        out_shape=[pltpu.VMEM(fields.shape, F32), pltpu.VMEM(frac.shape, F32)],
        in_specs=[hbm] * 4,
        out_specs=[vmem, vmem],
        scratch_shapes=[
            pltpu.SMEM(depth.shape, jnp.int32),
            pltpu.VMEM(fields.shape, F32), pltpu.VMEM(frac.shape, F32), pltpu.VMEM(helm.shape, F32),
            *[pltpu.VMEM(t, F32) for t in sent],
            *[pltpu.VMEM(t, F32) for t in sent],
            pltpu.VMEM((3, 2, lev, tall, clon), F32),
            pltpu.VMEM((2, lev, tall, clon), F32),
            pltpu.VMEM((lev, clat + BAND, clon), F32),
            pltpu.VMEM((2, lev, clat + BAND, clon), F32),
            pltpu.VMEM((4, *frac.shape), F32),
            pltpu.SemaphoreType.DMA((4,)),
            pltpu.SemaphoreType.DMA((12,)),
            pltpu.SemaphoreType.DMA((12,)),
        ],
        compiler_params=pltpu.CompilerParams(collective_id=0, has_side_effects=True, vmem_limit_bytes=24 << 20),
        name="step",
    )(*[pltpu.with_memory_space_constraint(x, pltpu.HBM) for x in (depth, fields, frac, helm)])
    return pl.pallas_call(
        store,
        out_shape=[jax.ShapeDtypeStruct(fields.shape, F32), jax.ShapeDtypeStruct(frac.shape, F32)],
        in_specs=[vmem, vmem],
        out_specs=[hbm, hbm],
        scratch_shapes=[pltpu.SemaphoreType.DMA((2,))],
        compiler_params=pltpu.CompilerParams(vmem_limit_bytes=1 << 20),
        name="store",
    )(*[pltpu.with_memory_space_constraint(x, pltpu.VMEM) for x in (departed, pressure)])


def solution(mesh):
    placed = (P(None, None, "lat", "lon"), P("lat"), P(None, "lat", "lon"), P(None, "lat", "lon"))
    return jax.shard_map(
        local,
        mesh=mesh,
        in_specs=placed,
        out_specs=(P(None, None, "lat", "lon"), P(None, "lat", "lon")),
        check_vma=False,
    )
```

```python
import functools

import jax
import jax.numpy as jnp
from jax import lax
from jax.experimental import pallas as pl
from jax.experimental.pallas import tpu as pltpu
from jax.sharding import PartitionSpec as P

BAND = 8
SHALLOW = 32
LANES = 128
NEAR = SHALLOW + 4
F32 = jnp.float32
MESH = pl.DeviceIdType.MESH
HALO_FIELDS = (0, 1, 3)
SPARE = 108


def turn(x, shift):
    shift %= LANES
    return x if shift == 0 else pltpu.roll(x, shift, axis=1)


def lane_of(shape):
    return lax.broadcasted_iota(jnp.int32, shape, len(shape) - 1)


def jet_band(depth_ref, bands):
    jet = jnp.int32(0)
    for b in range(1, bands):
        jet = jnp.where(depth_ref[b * BAND] > SHALLOW, b, jet)
    return jet


def interp_weights(frac):
    s = -frac
    below, above = (s - 1.0) * s, (s + 1.0) * (s + 2.0)
    return [
        s * above * (1.0 / 6.0),
        (s - 1.0) * above * -0.5,
        below * (s + 2.0) * 0.5,
        below * (s + 1.0) * (-1.0 / 6.0),
    ]


def depart(own, left, right, depth, weights):
    lane = lane_of(own[0].shape)
    totals = [jnp.zeros_like(own[0]) for _ in own]
    for o, w in zip((-1, 0, 1, 2), weights):
        s = depth + o
        t = lane + s
        shift = (s + LANES) & (LANES - 1)
        for n in range(len(own)):
            x = jnp.where(t <= LANES - 1, own[n], left[n])
            if o == -1:
                x = jnp.where(t == -1, right[n], x)
            totals[n] = totals[n] + w * pltpu.roll(x, shift, axis=1)
    return totals


def depart_beside(own, left, right, depth, weights):
    lane = lane_of(own[0].shape)
    totals = [jnp.zeros_like(own[0]) for _ in own]
    for o, w in zip((-1, 0, 1, 2), weights):
        s = depth + o
        t = lane + s
        shift = (s + LANES) & (LANES - 1)
        for n in range(len(own)):
            x = jnp.where(t <= LANES - 1, left[n], own[n])
            if o < 2:
                x = jnp.where((t >= 0) & (t <= 1), right[n], x)
            if o == -1:
                x = jnp.where(t == -1, own[n], x)
            totals[n] = totals[n] + w * pltpu.roll(x, shift, axis=1)
    return totals


def beside_pair(own, halo):
    lane = lane_of(own.shape)
    first, last = lane == 0, lane == LANES - 1
    return (
        (turn(jnp.where(first, halo, own), -1), turn(jnp.where(last, halo, own), 1)),
        (turn(jnp.where(first, own, halo), -1), turn(jnp.where(last, own, halo), 1)),
    )


ORDER = (0, 1, 3, 2, 4)


def whole_step(lev, clat, depth_hbm, fields_hbm, frac_hbm, helm_hbm, departed, pressure,
               depth_ref, fields, frac, helm, main, edge, top, bottom, dtop, dbottom, gtop, gbottom,
               main_i, edge_i, above, below, la, lb, ra, rb,
               ext, hel, rhs_s, p1_s, wts, in_sem, send_sem, recv_sem, ready_sem):
    bands = clat // BAND
    loads = [
        pltpu.make_async_copy(src, dst, in_sem.at[i])
        for i, (src, dst) in enumerate(
            ((depth_hbm, depth_ref), (frac_hbm, frac), (helm_hbm, helm),
             *[(fields_hbm.at[f], fields.at[f]) for f in ORDER]))
    ]
    for load in loads:
        load.start()
    nlon, nlat = lax.axis_size("lon"), lax.axis_size("lat")
    i, j = lax.axis_index("lon"), lax.axis_index("lat")
    east, west = lax.rem(i + 1, nlon), lax.rem(i + nlon - 1, nlon)
    south, north = j + 1, j - 1
    upper, lower = j > 0, j < nlat - 1
    rows_beyond = upper.astype(jnp.int32) + lower.astype(jnp.int32)
    peers = [{"lon": a, "lat": b} for a, b in (
        (east, j), (west, j), (i, north), (i, south),
        (east, north), (east, south), (west, north), (west, south))]

    def greet(semaphore, side, up, down):
        pl.semaphore_signal(semaphore, inc=1, device_id=peers[side], device_id_type=MESH)
        for there, peer in ((upper, up), (lower, down)):
            @pl.when(there)
            def _():
                pl.semaphore_signal(semaphore, inc=1, device_id=peers[peer], device_id_type=MESH)

    first, last = i == 0, i == nlon - 1
    second = i == 1
    barrier = pltpu.get_barrier_semaphore()
    greet(barrier, 0, 4, 5)

    @pl.when(jnp.logical_not(second))
    def _():
        greet(barrier, 1, 6, 7)

    for there, peer in ((upper, 2), (lower, 3)):
        @pl.when(there)
        def _():
            pl.semaphore_signal(barrier, inc=1, device_id=peers[peer], device_id_type=MESH)

    def copy(n, src, dst, peer):
        return pltpu.make_async_remote_copy(
            src_ref=src, dst_ref=dst, send_sem=send_sem.at[n], recv_sem=recv_sem.at[n],
            device_id=peers[peer], device_id_type=MESH)

    mains = {f: copy(7 + f, main.at[f], main_i.at[f], 0) for f in range(5)}
    west_copy = copy(0, edge, edge_i, 1)
    beyond = [
        copy(1, top, below, 2),
        copy(2, bottom, above, 3),
        copy(3, dtop, lb, 4),
        copy(4, dbottom, la, 5),
        copy(5, gtop, rb, 6),
        copy(6, gbottom, ra, 7),
    ]
    def westward():
        west_copy.start()
        for n in range(2):
            @pl.when((upper, lower)[n])
            def _():
                beyond[n].start()
                beyond[4 + n].start()

    for load in loads[:4]:
        load.wait()
    jet = jet_band(depth_ref, bands)
    nk = lev * BAND
    lane = lane_of((nk, LANES))
    jets = jnp.full((nk, LANES), jet)
    rest = None
    for b in range(bands):
        at = SPARE + 3 * b
        rows = pl.ds(b * BAND, BAND)
        fr = turn(frac[:, rows, :].reshape(nk, LANES), at - (LANES - 2))
        he = turn(helm[:, rows, :].reshape(nk, LANES), at + 2 - (LANES - 1))
        rest = fr if rest is None else jnp.where(lane >= at, fr, rest)
        rest = jnp.where(lane >= at + 2, he, rest)
    for f in ORDER:
        x = [fields[f, :, pl.ds(b * BAND, BAND), :].reshape(nk, LANES) for b in range(bands)]
        deep = x[0]
        for b in range(1, bands):
            deep = jnp.where(jets == b, x[b], deep)
        packed = None
        for slot in range(bands - 1):
            y = jnp.where(jets > slot, x[slot], x[slot + 1])
            y = turn(y, slot * NEAR + NEAR - LANES)
            packed = y if packed is None else jnp.where(lane >= slot * NEAR, y, packed)
        if f == 0:
            packed = jnp.where(lane >= SPARE, rest, packed)
        main[f, 0] = deep.reshape(lev, BAND, LANES)
        main[f, 1] = packed.reshape(lev, BAND, LANES)
        if f != ORDER[0]:
            mains[f].start()
        else:
            @pl.when(last)
            def _():
                pl.semaphore_wait(barrier, 2 + 3 * rows_beyond)
                mains[f].start()

            for load in loads[4:]:
                load.wait()
            acc = jnp.zeros((nk, LANES), F32)
            for b in range(bands):
                rows = pl.ds(b * BAND, BAND)
                for n in range(7):
                    src = fields[n, :, rows, :] if n < 5 else (frac if n == 5 else helm)[:, rows, :]
                    at = 32 * b + (17 if n == 6 else 3 * n)
                    acc = jnp.where(lane >= at, turn(src.reshape(nk, LANES), at), acc)
            edge[...] = acc.reshape(lev, BAND, LANES)
            lane8 = lane_of((2 * lev, LANES))
            for row, mine, diag, thin, n, at_depth in (
                    (0, top, dtop, gtop, 0, 0), (clat - 2, bottom, dbottom, gbottom, 1, clat - 1)):
                for q in range(5):
                    src = fields.at[HALO_FIELDS[q]] if q < 3 else (frac if q == 3 else helm)
                    for k in range(lev):
                        mine[q, 2 * k:2 * k + 2, :] = src[k, row:row + 2, :]
                mine[5] = jnp.full((2 * lev, LANES), depth_ref[at_depth].astype(F32))
                u = jnp.where(lane8 < 2, turn(mine[3], 2), mine[0])
                diag[0] = jnp.where(lane8 == 2, turn(mine[4], 3), u)
                diag[1] = mine[1]
                diag[2] = mine[2]
                g = mine[0]
                for q in range(1, 5):
                    at = 11 if q == 4 else 3 * q
                    g = jnp.where(lane8 >= at, turn(mine[q], at), g)
                thin[...] = g

                @pl.when(jnp.logical_not((upper, lower)[n]))
                def _():
                    for land in ((above, la, ra), (below, lb, rb))[n]:
                        land[...] = jnp.zeros_like(land)
            @pl.when(jnp.logical_not(first | last))
            def _():
                pl.semaphore_wait(barrier, 2 + 3 * rows_beyond)

            @pl.when(second)
            def _():
                greet(ready_sem, 1, 6, 7)

            @pl.when(first)
            def _():
                pl.semaphore_wait(ready_sem, 1 + rows_beyond)

            @pl.when(jnp.logical_not(first))
            def _():
                westward()

            for n in range(2):
                @pl.when((upper, lower)[n])
                def _():
                    beyond[2 + n].start()

            @pl.when(jnp.logical_not(last))
            def _():
                mains[f].start()

    @pl.when(first)
    def _():
        pl.semaphore_wait(barrier, 1 + 2 * rows_beyond)
        westward()

    for k in range(lev):
        for o, w in enumerate(interp_weights(frac[k])):
            wts[o, k] = w
        hel[0, k, pl.ds(BAND, clat), :] = helm[k]
    inside = (upper, lower)
    flat = lambda x: x.reshape(nk, LANES)
    tall3 = lambda x: x.reshape(lev, BAND, LANES)
    west_copy.wait_recv()
    for f in ORDER:
        mains[f].wait_recv()
        for b in range(bands):
            rows = pl.ds(b * BAND, BAND)
            depth = depth_ref[b * BAND]
            slot = b - (b > jet).astype(jnp.int32)
            amount = (2 * LANES - NEAR - NEAR * slot) & (LANES - 1)
            own = flat(fields[f, :, rows, :])
            left = jnp.where(jets == b, flat(main_i[f, 0]), pltpu.roll(flat(main_i[f, 1]), amount, axis=1))
            brim = flat(edge_i[...])
            right = turn(brim, -(32 * b + 3 * f))
            [got] = depart([own], [left], [right], depth, [flat(wts[o, :, rows, :]) for o in range(4)])
            departed[f, :, rows, :] = tall3(got)
            if f in HALO_FIELDS:
                q = HALO_FIELDS.index(f)
                rest = flat(main_i[0, 1])
                fr = jnp.where(lane < 64, turn(brim, -(32 * b + 15)), turn(rest, 18 - 3 * b))
                [past] = depart_beside([own], [left], [right], depth, interp_weights(fr))
                at = pl.ds((b + 1) * BAND, BAND)
                ext[q, 0, :, at, :] = tall3(got)
                ext[q, 1, :, at, :] = tall3(past)
                if f == 0:
                    he = jnp.where(lane < 64, turn(brim, -(32 * b + 17)), turn(rest, 17 - 3 * b))
                    hel[1, :, at, :] = tall3(he)
        if f == ORDER[2]:
            for n, c in enumerate(beyond):
                @pl.when((lower, upper)[n % 2])
                def _():
                    c.wait_recv()
            solve(lev, clat, inside, helm, above, below, la, lb, ra, rb, ext, hel, rhs_s, p1_s, pressure)
    for n, c in enumerate(beyond):
        @pl.when((upper, lower)[n % 2])
        def _():
            c.wait_send()
    for c in (west_copy, *mains.values()):
        c.wait_send()


def solve(lev, clat, inside, helm, above, below, la, lb, ra, rb, ext, hel, rhs_s, p1_s, pressure):
    lane = lane_of((BAND, LANES))
    for side, (mine, diag, thin) in enumerate(((above, la, ra), (below, lb, rb))):
        depth = jnp.max(mine[5]).astype(jnp.int32)
        own = [mine[q] for q in range(3)]
        left = [diag[q] for q in range(3)]
        g = thin[...]
        right = [turn(g, -3 * q) for q in range(3)]
        fr = jnp.where(lane < 64, turn(g, -9), turn(left[0], -2))
        he = jnp.where(lane < 64, turn(g, -11), turn(left[0], -3))
        got = depart(own, left, right, depth, interp_weights(mine[3]))
        past = depart_beside(own, left, right, depth, interp_weights(fr))
        at = BAND - 2 if side == 0 else BAND + clat
        for k in range(lev):
            pair = slice(2 * k, 2 * k + 2)
            for q in range(3):
                ext[q, 0, k, at:at + 2, :] = jnp.where(inside[side], got[q], 0.0)[pair]
                ext[q, 1, k, at:at + 2, :] = jnp.where(inside[side], past[q], 0.0)[pair]
            hel[0, k, at:at + 2, :] = mine[4][pair]
            hel[1, k, at:at + 2, :] = he[pair]
    tall = clat + BAND
    row = lax.broadcasted_iota(jnp.int32, (lev, tall, LANES), 1)
    outside = ((row == 0) & jnp.logical_not(inside[0])) | ((row == clat + 1) & jnp.logical_not(inside[1]))
    first = BAND - 1
    flat = lambda x: x.reshape(-1, LANES)
    mid, up, down = pl.ds(first, tall), pl.ds(first - 1, tall), pl.ds(first + 1, tall)
    u_all = beside_pair(flat(ext[0, 0, :, mid, :]), flat(ext[0, 1, :, mid, :]))
    phi = [flat(ext[2, h, :, mid, :]) for h in range(2)]
    phi_all = beside_pair(*phi)
    for h in range(2):
        div = 0.5 * (u_all[h][0] - u_all[h][1] + flat(ext[1, h, :, down, :]) - flat(ext[1, h, :, up, :]))
        rhs = phi[h] - 0.5 * div
        around = phi_all[h][0] + phi_all[h][1] + flat(ext[2, h, :, down, :]) + flat(ext[2, h, :, up, :])
        p1 = (rhs + around) / (4.0 + flat(hel[h, :, mid, :]))
        p1_s[h] = jnp.where(outside, 0.0, p1.reshape(lev, tall, LANES))
        if h == 0:
            rhs_s[...] = rhs.reshape(lev, tall, LANES)
    mid = pl.ds(1, clat)
    east, west = beside_pair(flat(p1_s[0, :, mid, :]), flat(p1_s[1, :, mid, :]))[0]
    around = east + west + flat(p1_s[0, :, pl.ds(2, clat), :]) + flat(p1_s[0, :, pl.ds(0, clat), :])
    pressure[...] = ((flat(rhs_s[:, mid, :]) + around) / (4.0 + flat(helm[...]))).reshape(lev, clat, LANES)


def store(departed, pressure, departed_o, pressure_o, sem):
    copies = [pltpu.make_async_copy(departed, departed_o, sem.at[0]), pltpu.make_async_copy(pressure, pressure_o, sem.at[1])]
    for c in copies:
        c.start()
    for c in copies:
        c.wait()


def local(fields, depth, frac, helm):
    lev, clat, clon = fields.shape[1:]
    hbm = pl.BlockSpec(memory_space=pltpu.HBM)
    vmem = pl.BlockSpec(memory_space=pltpu.VMEM)
    sent = [(5, 2, lev, BAND, clon), (lev, BAND, clon), (6, 2 * lev, clon), (6, 2 * lev, clon),
            (3, 2 * lev, clon), (3, 2 * lev, clon), (2 * lev, clon), (2 * lev, clon)]
    tall = clat + 2 * BAND
    departed, pressure = pl.pallas_call(
        functools.partial(whole_step, lev, clat),
        out_shape=[pltpu.VMEM(fields.shape, F32), pltpu.VMEM(frac.shape, F32)],
        in_specs=[hbm] * 4,
        out_specs=[vmem, vmem],
        scratch_shapes=[
            pltpu.SMEM(depth.shape, jnp.int32),
            pltpu.VMEM(fields.shape, F32), pltpu.VMEM(frac.shape, F32), pltpu.VMEM(helm.shape, F32),
            *[pltpu.VMEM(t, F32) for t in sent],
            *[pltpu.VMEM(t, F32) for t in sent],
            pltpu.VMEM((3, 2, lev, tall, clon), F32),
            pltpu.VMEM((2, lev, tall, clon), F32),
            pltpu.VMEM((lev, clat + BAND, clon), F32),
            pltpu.VMEM((2, lev, clat + BAND, clon), F32),
            pltpu.VMEM((4, *frac.shape), F32),
            pltpu.SemaphoreType.DMA((8,)),
            pltpu.SemaphoreType.DMA((12,)),
            pltpu.SemaphoreType.DMA((12,)),
            pltpu.SemaphoreType.REGULAR,
        ],
        compiler_params=pltpu.CompilerParams(collective_id=0, has_side_effects=True, vmem_limit_bytes=24 << 20),
        name="step",
    )(*[pltpu.with_memory_space_constraint(x, pltpu.HBM) for x in (depth, fields, frac, helm)])
    return pl.pallas_call(
        store,
        out_shape=[jax.ShapeDtypeStruct(fields.shape, F32), jax.ShapeDtypeStruct(frac.shape, F32)],
        in_specs=[vmem, vmem],
        out_specs=[hbm, hbm],
        scratch_shapes=[pltpu.SemaphoreType.DMA((2,))],
        compiler_params=pltpu.CompilerParams(vmem_limit_bytes=1 << 20),
        name="store",
    )(*[pltpu.with_memory_space_constraint(x, pltpu.VMEM) for x in (departed, pressure)])


def solution(mesh):
    placed = (P(None, None, "lat", "lon"), P("lat"), P(None, "lat", "lon"), P(None, "lat", "lon"))
    return jax.shard_map(
        local,
        mesh=mesh,
        in_specs=placed,
        out_specs=(P(None, None, "lat", "lon"), P(None, "lat", "lon")),
        check_vma=False,
    )
```

```python
import functools

import jax
import jax.numpy as jnp
from jax import lax
from jax.experimental import pallas as pl
from jax.experimental.pallas import tpu as pltpu
from jax.sharding import PartitionSpec as P

BAND = 8
SHALLOW = 32
LANES = 128
NEAR = SHALLOW + 4
F32 = jnp.float32
MESH = pl.DeviceIdType.MESH
HALO_FIELDS = (0, 1, 3)
SPARE = 108
FILL = 28
PER_TILE = 3
REST = ((0, 108), (1, 108), (2, 104), (2, 116))


def turn(x, shift):
    shift %= LANES
    return x if shift == 0 else pltpu.roll(x, shift, axis=1)


def lane_of(shape):
    return lax.broadcasted_iota(jnp.int32, shape, len(shape) - 1)


def jet_band(depth_ref, bands):
    jet = jnp.int32(0)
    for b in range(1, bands):
        jet = jnp.where(depth_ref[b * BAND] > SHALLOW, b, jet)
    return jet


def interp_weights(frac):
    s = -frac
    below, above = (s - 1.0) * s, (s + 1.0) * (s + 2.0)
    return [
        s * above * (1.0 / 6.0),
        (s - 1.0) * above * -0.5,
        below * (s + 2.0) * 0.5,
        below * (s + 1.0) * (-1.0 / 6.0),
    ]


def depart(own, left, right, depth, weights):
    lane = lane_of(own[0].shape)
    totals = [jnp.zeros_like(own[0]) for _ in own]
    for o, w in zip((-1, 0, 1, 2), weights):
        s = depth + o
        t = lane + s
        shift = (s + LANES) & (LANES - 1)
        for n in range(len(own)):
            x = jnp.where(t <= LANES - 1, own[n], left[n])
            if o == -1:
                x = jnp.where(t == -1, right[n], x)
            totals[n] = totals[n] + w * pltpu.roll(x, shift, axis=1)
    return totals


def depart_beside(own, left, right, depth, weights):
    lane = lane_of(own[0].shape)
    totals = [jnp.zeros_like(own[0]) for _ in own]
    for o, w in zip((-1, 0, 1, 2), weights):
        s = depth + o
        t = lane + s
        shift = (s + LANES) & (LANES - 1)
        for n in range(len(own)):
            x = jnp.where(t <= LANES - 1, left[n], own[n])
            if o < 2:
                x = jnp.where((t >= 0) & (t <= 1), right[n], x)
            if o == -1:
                x = jnp.where(t == -1, own[n], x)
            totals[n] = totals[n] + w * pltpu.roll(x, shift, axis=1)
    return totals


def beside_pair(own, halo):
    lane = lane_of(own.shape)
    first, last = lane == 0, lane == LANES - 1
    return (
        (turn(jnp.where(first, halo, own), -1), turn(jnp.where(last, halo, own), 1)),
        (turn(jnp.where(first, own, halo), -1), turn(jnp.where(last, own, halo), 1)),
    )


ORDER = (0, 1, 3, 2, 4)


def whole_step(lev, clat, depth_hbm, fields_hbm, frac_hbm, helm_hbm, departed, pressure,
               depth_ref, fields, frac, helm, main, edge, top, bottom, dtop, dbottom, gtop, gbottom,
               main_i, edge_i, above, below, la, lb, ra, rb,
               ext, hel, rhs_s, p1_s, wts, wts2, in_sem, send_sem, recv_sem, ready_sem):
    bands = clat // BAND
    loads = [
        pltpu.make_async_copy(src, dst, in_sem.at[i])
        for i, (src, dst) in enumerate(
            ((depth_hbm, depth_ref), (frac_hbm, frac), (helm_hbm, helm),
             *[(fields_hbm.at[f], fields.at[f]) for f in ORDER]))
    ]
    for n in (0, 3, 4, 5, 1, 2, 6, 7):
        loads[n].start()
    nlon, nlat = lax.axis_size("lon"), lax.axis_size("lat")
    i, j = lax.axis_index("lon"), lax.axis_index("lat")
    east, west = lax.rem(i + 1, nlon), lax.rem(i + nlon - 1, nlon)
    south, north = j + 1, j - 1
    upper, lower = j > 0, j < nlat - 1
    rows_beyond = upper.astype(jnp.int32) + lower.astype(jnp.int32)
    peers = [{"lon": a, "lat": b} for a, b in (
        (east, j), (west, j), (i, north), (i, south),
        (east, north), (east, south), (west, north), (west, south))]

    def greet(semaphore, side, up, down):
        pl.semaphore_signal(semaphore, inc=1, device_id=peers[side], device_id_type=MESH)
        for there, peer in ((upper, up), (lower, down)):
            @pl.when(there)
            def _():
                pl.semaphore_signal(semaphore, inc=1, device_id=peers[peer], device_id_type=MESH)

    first, last = i == 0, i == nlon - 1
    second = i == 1
    barrier = pltpu.get_barrier_semaphore()
    greet(barrier, 0, 4, 5)

    @pl.when(jnp.logical_not(second))
    def _():
        greet(barrier, 1, 6, 7)

    for there, peer in ((upper, 2), (lower, 3)):
        @pl.when(there)
        def _():
            pl.semaphore_signal(barrier, inc=1, device_id=peers[peer], device_id_type=MESH)

    def copy(n, src, dst, peer):
        return pltpu.make_async_remote_copy(
            src_ref=src, dst_ref=dst, send_sem=send_sem.at[n], recv_sem=recv_sem.at[n],
            device_id=peers[peer], device_id_type=MESH)

    mains = {f: copy(7 + f, main.at[f], main_i.at[f], 0) for f in range(5)}
    west_copy = copy(0, edge, edge_i, 1)
    beyond = [
        copy(1, top, below, 2),
        copy(2, bottom, above, 3),
        copy(3, dtop, lb, 4),
        copy(4, dbottom, la, 5),
        copy(5, gtop, rb, 6),
        copy(6, gbottom, ra, 7),
    ]
    def westward():
        west_copy.start()
        for n in range(2):
            @pl.when((upper, lower)[n])
            def _():
                beyond[n].start()
                beyond[4 + n].start()

    for load in (loads[0], loads[3]):
        load.wait()
    jet = jet_band(depth_ref, bands)
    nk = lev * BAND
    lane = lane_of((nk, LANES))
    jets = jnp.full((nk, LANES), jet)
    thin_lane = lane_of((BAND, LANES))
    last_slot = bands - 2
    pieces = [(slot, k) for k in range(lev) for slot in range(last_slot)]
    tail = len(pieces) % PER_TILE * NEAR

    def level(x, k):
        return x[k * BAND:(k + 1) * BAND]

    for f in ORDER:
        if f == ORDER[1]:
            rest = None
            for b in range(bands):
                at = SPARE + 3 * b
                rows = pl.ds(b * BAND, BAND)
                fr = turn(frac[:, rows, :].reshape(nk, LANES), at - (LANES - 2))
                he = turn(helm[:, rows, :].reshape(nk, LANES), at + 2 - (LANES - 1))
                rest = fr if rest is None else jnp.where(lane >= at, fr, rest)
                rest = jnp.where(lane >= at + 2, he, rest)
        x = [fields[f, :, pl.ds(b * BAND, BAND), :].reshape(nk, LANES) for b in range(bands)]
        deep = x[0]
        for b in range(1, bands):
            deep = jnp.where(jets == b, x[b], deep)
        slots = [jnp.where(jets > slot, x[slot], x[slot + 1]) for slot in range(bands - 1)]
        deep = jnp.where(lane < FILL, turn(slots[last_slot], FILL), deep)
        main[f, 0:lev] = deep.reshape(lev, BAND, LANES)
        packed = []
        for n, (slot, k) in enumerate(pieces):
            at = n % PER_TILE * NEAR
            y = turn(level(slots[slot], k), at + NEAR - LANES)
            if at == 0:
                packed.append(y)
            else:
                packed[-1] = jnp.where(thin_lane >= at, y, packed[-1])
        for k in range(lev):
            at = tail + (NEAR - FILL) * k
            packed[-1] = jnp.where(thin_lane >= at, turn(level(slots[last_slot], k), at + NEAR - LANES), packed[-1])
        if f == ORDER[1]:
            for k, (tile, at) in enumerate(REST):
                packed[tile] = jnp.where(thin_lane >= at, turn(level(rest, k), at - SPARE), packed[tile])
        for n, y in enumerate(packed):
            main[f, lev + n] = y
        if f != ORDER[0]:
            mains[f].start()
        else:
            @pl.when(last)
            def _():
                pl.semaphore_wait(barrier, 2 + 3 * rows_beyond)
                mains[f].start()

            for load in (*loads[1:3], *loads[4:]):
                load.wait()
            acc = jnp.zeros((nk, LANES), F32)
            for b in range(bands):
                rows = pl.ds(b * BAND, BAND)
                for n in range(7):
                    src = fields[n, :, rows, :] if n < 5 else (frac if n == 5 else helm)[:, rows, :]
                    at = 32 * b + (17 if n == 6 else 3 * n)
                    acc = jnp.where(lane >= at, turn(src.reshape(nk, LANES), at), acc)
            edge[...] = acc.reshape(lev, BAND, LANES)
            lane8 = lane_of((2 * lev, LANES))
            for row, mine, diag, thin, n, at_depth in (
                    (0, top, dtop, gtop, 0, 0), (clat - 2, bottom, dbottom, gbottom, 1, clat - 1)):
                for q in range(5):
                    src = fields.at[HALO_FIELDS[q]] if q < 3 else (frac if q == 3 else helm)
                    for k in range(lev):
                        mine[q, 2 * k:2 * k + 2, :] = src[k, row:row + 2, :]
                mine[5] = jnp.full((2 * lev, LANES), depth_ref[at_depth].astype(F32))
                u = jnp.where(lane8 < 2, turn(mine[3], 2), mine[0])
                diag[0] = jnp.where(lane8 == 2, turn(mine[4], 3), u)
                diag[1] = mine[1]
                diag[2] = mine[2]
                g = mine[0]
                for q in range(1, 5):
                    at = 11 if q == 4 else 3 * q
                    g = jnp.where(lane8 >= at, turn(mine[q], at), g)
                thin[...] = g

                @pl.when(jnp.logical_not((upper, lower)[n]))
                def _():
                    for land in ((above, la, ra), (below, lb, rb))[n]:
                        land[...] = jnp.zeros_like(land)
            @pl.when(jnp.logical_not(first | last))
            def _():
                pl.semaphore_wait(barrier, 2 + 3 * rows_beyond)

            @pl.when(second)
            def _():
                greet(ready_sem, 1, 6, 7)

            @pl.when(first)
            def _():
                pl.semaphore_wait(ready_sem, 1 + rows_beyond)

            @pl.when(jnp.logical_not(first))
            def _():
                westward()

            for n in range(2):
                @pl.when((upper, lower)[n])
                def _():
                    beyond[2 + n].start()

            @pl.when(jnp.logical_not(last))
            def _():
                mains[f].start()

    @pl.when(first)
    def _():
        pl.semaphore_wait(barrier, 1 + 2 * rows_beyond)
        westward()

    for k in range(lev):
        for o, w in enumerate(interp_weights(frac[k])):
            wts[o, k] = w
        hel[0, k, pl.ds(BAND, clat), :] = helm[k]
    inside = (upper, lower)
    flat = lambda x: x.reshape(nk, LANES)
    tall3 = lambda x: x.reshape(lev, BAND, LANES)
    west_copy.wait_recv()
    brim = flat(edge_i[...])

    def parts(f):
        tiles = [main_i[f, n] for n in range(main_i.shape[1])]
        near = [
            jnp.concatenate(
                [turn(tiles[lev + n // PER_TILE], LANES - NEAR - n % PER_TILE * NEAR)
                 for n in range(slot, len(pieces), last_slot)], axis=0)
            for slot in range(last_slot)
        ]
        near.append(jnp.concatenate(
            [jnp.where(thin_lane >= LANES - FILL, turn(tiles[k], -FILL),
                       turn(tiles[-1], LANES - NEAR - tail - (NEAR - FILL) * k)) for k in range(lev)], axis=0))
        deep = jnp.concatenate(tiles[:lev], axis=0)
        for b in range(bands):
            left = near[min(b, last_slot)]
            if 0 < b <= last_slot:
                left = jnp.where(jets < b, near[b - 1], left)
            yield (flat(fields[f, :, pl.ds(b * BAND, BAND), :]), jnp.where(jets == b, deep, left),
                   turn(brim, -(32 * b + 3 * f)), depth_ref[b * BAND])

    for f in ORDER:
        mains[f].wait_recv()
        for b, (own, left, right, depth) in enumerate(parts(f)):
            rows = pl.ds(b * BAND, BAND)
            [got] = depart([own], [left], [right], depth, [flat(wts[o, :, rows, :]) for o in range(4)])
            departed[f, :, rows, :] = tall3(got)
            if f in HALO_FIELDS:
                ext[HALO_FIELDS.index(f), 0, :, pl.ds((b + 1) * BAND, BAND), :] = tall3(got)
        if f == ORDER[1]:
            rest = jnp.concatenate([turn(main_i[f, lev + tile], SPARE - at) for tile, at in REST], axis=0)
            for b in range(bands):
                rows = pl.ds(b * BAND, BAND)
                fr = jnp.where(lane < 64, turn(brim, -(32 * b + 15)), turn(rest, 18 - 3 * b))
                he = jnp.where(lane < 64, turn(brim, -(32 * b + 17)), turn(rest, 17 - 3 * b))
                for o, w in enumerate(interp_weights(fr)):
                    wts2[o, :, rows, :] = tall3(w)
                hel[1, :, pl.ds((b + 1) * BAND, BAND), :] = tall3(he)
        for g in {ORDER[1]: ORDER[:2], ORDER[2]: ORDER[2:3]}.get(f, ()):
            for b, (own, left, right, depth) in enumerate(parts(g)):
                rows = pl.ds(b * BAND, BAND)
                [past] = depart_beside([own], [left], [right], depth, [flat(wts2[o, :, rows, :]) for o in range(4)])
                ext[HALO_FIELDS.index(g), 1, :, pl.ds((b + 1) * BAND, BAND), :] = tall3(past)
        if f == ORDER[2]:
            for n, c in enumerate(beyond):
                @pl.when((lower, upper)[n % 2])
                def _():
                    c.wait_recv()
            solve(lev, clat, inside, helm, above, below, la, lb, ra, rb, ext, hel, rhs_s, p1_s, pressure)
    for n, c in enumerate(beyond):
        @pl.when((upper, lower)[n % 2])
        def _():
            c.wait_send()
    for c in (west_copy, *mains.values()):
        c.wait_send()


def solve(lev, clat, inside, helm, above, below, la, lb, ra, rb, ext, hel, rhs_s, p1_s, pressure):
    lane = lane_of((BAND, LANES))
    for side, (mine, diag, thin) in enumerate(((above, la, ra), (below, lb, rb))):
        depth = jnp.max(mine[5]).astype(jnp.int32)
        own = [mine[q] for q in range(3)]
        left = [diag[q] for q in range(3)]
        g = thin[...]
        right = [turn(g, -3 * q) for q in range(3)]
        fr = jnp.where(lane < 64, turn(g, -9), turn(left[0], -2))
        he = jnp.where(lane < 64, turn(g, -11), turn(left[0], -3))
        got = depart(own, left, right, depth, interp_weights(mine[3]))
        past = depart_beside(own, left, right, depth, interp_weights(fr))
        at = BAND - 2 if side == 0 else BAND + clat
        for k in range(lev):
            pair = slice(2 * k, 2 * k + 2)
            for q in range(3):
                ext[q, 0, k, at:at + 2, :] = jnp.where(inside[side], got[q], 0.0)[pair]
                ext[q, 1, k, at:at + 2, :] = jnp.where(inside[side], past[q], 0.0)[pair]
            hel[0, k, at:at + 2, :] = mine[4][pair]
            hel[1, k, at:at + 2, :] = he[pair]
    tall = clat + BAND
    row = lax.broadcasted_iota(jnp.int32, (lev, tall, LANES), 1)
    outside = ((row == 0) & jnp.logical_not(inside[0])) | ((row == clat + 1) & jnp.logical_not(inside[1]))
    first = BAND - 1
    flat = lambda x: x.reshape(-1, LANES)
    mid, up, down = pl.ds(first, tall), pl.ds(first - 1, tall), pl.ds(first + 1, tall)
    u_all = beside_pair(flat(ext[0, 0, :, mid, :]), flat(ext[0, 1, :, mid, :]))
    phi = [flat(ext[2, h, :, mid, :]) for h in range(2)]
    phi_all = beside_pair(*phi)
    for h in range(2):
        div = 0.5 * (u_all[h][0] - u_all[h][1] + flat(ext[1, h, :, down, :]) - flat(ext[1, h, :, up, :]))
        rhs = phi[h] - 0.5 * div
        around = phi_all[h][0] + phi_all[h][1] + flat(ext[2, h, :, down, :]) + flat(ext[2, h, :, up, :])
        p1 = (rhs + around) / (4.0 + flat(hel[h, :, mid, :]))
        p1_s[h] = jnp.where(outside, 0.0, p1.reshape(lev, tall, LANES))
        if h == 0:
            rhs_s[...] = rhs.reshape(lev, tall, LANES)
    mid = pl.ds(1, clat)
    east, west = beside_pair(flat(p1_s[0, :, mid, :]), flat(p1_s[1, :, mid, :]))[0]
    around = east + west + flat(p1_s[0, :, pl.ds(2, clat), :]) + flat(p1_s[0, :, pl.ds(0, clat), :])
    pressure[...] = ((flat(rhs_s[:, mid, :]) + around) / (4.0 + flat(helm[...]))).reshape(lev, clat, LANES)


def store(departed, pressure, departed_o, pressure_o, sem):
    copies = [pltpu.make_async_copy(departed, departed_o, sem.at[0]), pltpu.make_async_copy(pressure, pressure_o, sem.at[1])]
    for c in copies:
        c.start()
    for c in copies:
        c.wait()


def local(fields, depth, frac, helm):
    lev, clat, clon = fields.shape[1:]
    hbm = pl.BlockSpec(memory_space=pltpu.HBM)
    vmem = pl.BlockSpec(memory_space=pltpu.VMEM)
    sent = [(5, lev + REST[-1][0] + 1, BAND, clon), (lev, BAND, clon), (6, 2 * lev, clon), (6, 2 * lev, clon),
            (3, 2 * lev, clon), (3, 2 * lev, clon), (2 * lev, clon), (2 * lev, clon)]
    tall = clat + 2 * BAND
    departed, pressure = pl.pallas_call(
        functools.partial(whole_step, lev, clat),
        out_shape=[pltpu.VMEM(fields.shape, F32), pltpu.VMEM(frac.shape, F32)],
        in_specs=[hbm] * 4,
        out_specs=[vmem, vmem],
        scratch_shapes=[
            pltpu.SMEM(depth.shape, jnp.int32),
            pltpu.VMEM(fields.shape, F32), pltpu.VMEM(frac.shape, F32), pltpu.VMEM(helm.shape, F32),
            *[pltpu.VMEM(t, F32) for t in sent],
            *[pltpu.VMEM(t, F32) for t in sent],
            pltpu.VMEM((3, 2, lev, tall, clon), F32),
            pltpu.VMEM((2, lev, tall, clon), F32),
            pltpu.VMEM((lev, clat + BAND, clon), F32),
            pltpu.VMEM((2, lev, clat + BAND, clon), F32),
            pltpu.VMEM((4, *frac.shape), F32),
            pltpu.VMEM((4, *frac.shape), F32),
            pltpu.SemaphoreType.DMA((8,)),
            pltpu.SemaphoreType.DMA((12,)),
            pltpu.SemaphoreType.DMA((12,)),
            pltpu.SemaphoreType.REGULAR,
        ],
        compiler_params=pltpu.CompilerParams(collective_id=0, has_side_effects=True, vmem_limit_bytes=24 << 20),
        name="step",
    )(*[pltpu.with_memory_space_constraint(x, pltpu.HBM) for x in (depth, fields, frac, helm)])
    return pl.pallas_call(
        store,
        out_shape=[jax.ShapeDtypeStruct(fields.shape, F32), jax.ShapeDtypeStruct(frac.shape, F32)],
        in_specs=[vmem, vmem],
        out_specs=[hbm, hbm],
        scratch_shapes=[pltpu.SemaphoreType.DMA((2,))],
        compiler_params=pltpu.CompilerParams(vmem_limit_bytes=1 << 20),
        name="store",
    )(*[pltpu.with_memory_space_constraint(x, pltpu.VMEM) for x in (departed, pressure)])


def solution(mesh):
    placed = (P(None, None, "lat", "lon"), P("lat"), P(None, "lat", "lon"), P(None, "lat", "lon"))
    return jax.shard_map(
        local,
        mesh=mesh,
        in_specs=placed,
        out_specs=(P(None, None, "lat", "lon"), P(None, "lat", "lon")),
        check_vma=False,
    )
```

```python
import functools

import jax
import jax.numpy as jnp
from jax import lax
from jax.experimental import pallas as pl
from jax.experimental.pallas import tpu as pltpu
from jax.sharding import PartitionSpec as P

BAND = 8
SHALLOW = 32
LANES = 128
NEAR = SHALLOW + 4
F32 = jnp.float32
MESH = pl.DeviceIdType.MESH
HALO_FIELDS = (0, 1, 3)
SPARE = 108
FILL = 28
PER_TILE = 3
REST = ((0, 108), (1, 108), (2, 104), (2, 116))


def turn(x, shift):
    shift %= LANES
    return x if shift == 0 else pltpu.roll(x, shift, axis=1)


def lane_of(shape):
    return lax.broadcasted_iota(jnp.int32, shape, len(shape) - 1)


def jet_band(depth_ref, bands):
    jet = jnp.int32(0)
    for b in range(1, bands):
        jet = jnp.where(depth_ref[b * BAND] > SHALLOW, b, jet)
    return jet


def interp_weights(frac):
    s = -frac
    below, above = (s - 1.0) * s, (s + 1.0) * (s + 2.0)
    return [
        s * above * (1.0 / 6.0),
        (s - 1.0) * above * -0.5,
        below * (s + 2.0) * 0.5,
        below * (s + 1.0) * (-1.0 / 6.0),
    ]


def depart(own, left, right, depth, weights):
    lane = lane_of(own[0].shape)
    totals = [jnp.zeros_like(own[0]) for _ in own]
    for o, w in zip((-1, 0, 1, 2), weights):
        s = depth + o
        t = lane + s
        shift = (s + LANES) & (LANES - 1)
        for n in range(len(own)):
            x = jnp.where(t <= LANES - 1, own[n], left[n])
            if o == -1:
                x = jnp.where(t == -1, right[n], x)
            totals[n] = totals[n] + w * pltpu.roll(x, shift, axis=1)
    return totals


def depart_beside(own, left, right, depth, weights):
    lane = lane_of(own[0].shape)
    totals = [jnp.zeros_like(own[0]) for _ in own]
    for o, w in zip((-1, 0, 1, 2), weights):
        s = depth + o
        t = lane + s
        shift = (s + LANES) & (LANES - 1)
        for n in range(len(own)):
            x = jnp.where(t <= LANES - 1, left[n], own[n])
            if o < 2:
                x = jnp.where((t >= 0) & (t <= 1), right[n], x)
            if o == -1:
                x = jnp.where(t == -1, own[n], x)
            totals[n] = totals[n] + w * pltpu.roll(x, shift, axis=1)
    return totals


def beside_pair(own, halo):
    lane = lane_of(own.shape)
    first, last = lane == 0, lane == LANES - 1
    return (
        (turn(jnp.where(first, halo, own), -1), turn(jnp.where(last, halo, own), 1)),
        (turn(jnp.where(first, own, halo), -1), turn(jnp.where(last, own, halo), 1)),
    )


ORDER = (0, 1, 3, 2, 4)


def whole_step(lev, clat, depth_hbm, fields_hbm, frac_hbm, helm_hbm, departed, pressure,
               depth_ref, fields, frac, helm, main, edge, top, bottom, dtop, dbottom, gtop, gbottom,
               main_i, edge_i, above, below, la, lb, ra, rb,
               ext, hel, rhs_s, p1_s, wts, brink, in_sem, send_sem, recv_sem, ready_sem):
    bands = clat // BAND
    loads = [
        pltpu.make_async_copy(src, dst, in_sem.at[i])
        for i, (src, dst) in enumerate(
            ((depth_hbm, depth_ref), (frac_hbm, frac), (helm_hbm, helm),
             *[(fields_hbm.at[f], fields.at[f]) for f in ORDER]))
    ]
    for n in (0, 3, 4, 5, 1, 2, 6, 7):
        loads[n].start()
    nlon, nlat = lax.axis_size("lon"), lax.axis_size("lat")
    i, j = lax.axis_index("lon"), lax.axis_index("lat")
    east, west = lax.rem(i + 1, nlon), lax.rem(i + nlon - 1, nlon)
    south, north = j + 1, j - 1
    upper, lower = j > 0, j < nlat - 1
    rows_beyond = upper.astype(jnp.int32) + lower.astype(jnp.int32)
    peers = [{"lon": a, "lat": b} for a, b in (
        (east, j), (west, j), (i, north), (i, south),
        (east, north), (east, south), (west, north), (west, south))]

    def greet(semaphore, side, up, down):
        pl.semaphore_signal(semaphore, inc=1, device_id=peers[side], device_id_type=MESH)
        for there, peer in ((upper, up), (lower, down)):
            @pl.when(there)
            def _():
                pl.semaphore_signal(semaphore, inc=1, device_id=peers[peer], device_id_type=MESH)

    first, last = i == 0, i == nlon - 1
    second = i == 1
    barrier = pltpu.get_barrier_semaphore()
    greet(barrier, 0, 4, 5)

    @pl.when(jnp.logical_not(second))
    def _():
        greet(barrier, 1, 6, 7)

    for there, peer in ((upper, 2), (lower, 3)):
        @pl.when(there)
        def _():
            pl.semaphore_signal(barrier, inc=1, device_id=peers[peer], device_id_type=MESH)

    def copy(n, src, dst, peer):
        return pltpu.make_async_remote_copy(
            src_ref=src, dst_ref=dst, send_sem=send_sem.at[n], recv_sem=recv_sem.at[n],
            device_id=peers[peer], device_id_type=MESH)

    mains = {f: copy(7 + f, main.at[f], main_i.at[f], 0) for f in range(5)}
    west_copy = copy(0, edge, edge_i, 1)
    beyond = [
        copy(1, top, below, 2),
        copy(2, bottom, above, 3),
        copy(3, dtop, lb, 4),
        copy(4, dbottom, la, 5),
        copy(5, gtop, rb, 6),
        copy(6, gbottom, ra, 7),
    ]
    def westward():
        west_copy.start()
        for n in range(2):
            @pl.when((upper, lower)[n])
            def _():
                beyond[n].start()
                beyond[4 + n].start()

    for load in (loads[0], loads[3]):
        load.wait()
    jet = jet_band(depth_ref, bands)
    nk = lev * BAND
    lane = lane_of((nk, LANES))
    jets = jnp.full((nk, LANES), jet)
    thin_lane = lane_of((BAND, LANES))
    last_slot = bands - 2
    pieces = [(slot, k) for k in range(lev) for slot in range(last_slot)]
    tail = len(pieces) % PER_TILE * NEAR

    def level(x, k):
        return x[k * BAND:(k + 1) * BAND]

    for f in ORDER:
        if f == ORDER[1]:
            for n in (4, 1, 2):
                loads[n].wait()
            rest = None
            for b in range(bands):
                at = SPARE + 3 * b
                rows = pl.ds(b * BAND, BAND)
                fr = turn(frac[:, rows, :].reshape(nk, LANES), at - (LANES - 2))
                he = turn(helm[:, rows, :].reshape(nk, LANES), at + 2 - (LANES - 1))
                rest = fr if rest is None else jnp.where(lane >= at, fr, rest)
                rest = jnp.where(lane >= at + 2, he, rest)
        if f == ORDER[2]:
            loads[5].wait()
        x = [fields[f, :, pl.ds(b * BAND, BAND), :].reshape(nk, LANES) for b in range(bands)]
        deep = x[0]
        for b in range(1, bands):
            deep = jnp.where(jets == b, x[b], deep)
        slots = [jnp.where(jets > slot, x[slot], x[slot + 1]) for slot in range(bands - 1)]
        deep = jnp.where(lane < FILL, turn(slots[last_slot], FILL), deep)
        main[f, 0:lev] = deep.reshape(lev, BAND, LANES)
        packed = []
        for n, (slot, k) in enumerate(pieces):
            at = n % PER_TILE * NEAR
            y = turn(level(slots[slot], k), at + NEAR - LANES)
            if at == 0:
                packed.append(y)
            else:
                packed[-1] = jnp.where(thin_lane >= at, y, packed[-1])
        for k in range(lev):
            at = tail + (NEAR - FILL) * k
            packed[-1] = jnp.where(thin_lane >= at, turn(level(slots[last_slot], k), at + NEAR - LANES), packed[-1])
        if f == ORDER[1]:
            for k, (tile, at) in enumerate(REST):
                packed[tile] = jnp.where(thin_lane >= at, turn(level(rest, k), at - SPARE), packed[tile])
        for n, y in enumerate(packed):
            main[f, lev + n] = y
        if f in ORDER[3:]:
            mains[f].start()
        else:
            @pl.when(last)
            def _():
                if f == ORDER[0]:
                    pl.semaphore_wait(barrier, 2 + 3 * rows_beyond)
                mains[f].start()

        if f == ORDER[2]:
            for n in (6, 7):
                loads[n].wait()
            acc = jnp.zeros((nk, LANES), F32)
            for b in range(bands):
                rows = pl.ds(b * BAND, BAND)
                for n in range(7):
                    src = fields[n, :, rows, :] if n < 5 else (frac if n == 5 else helm)[:, rows, :]
                    at = 32 * b + (17 if n == 6 else 3 * n)
                    acc = jnp.where(lane >= at, turn(src.reshape(nk, LANES), at), acc)
            edge[...] = acc.reshape(lev, BAND, LANES)
            lane8 = lane_of((2 * lev, LANES))
            for row, mine, diag, thin, n, at_depth in (
                    (0, top, dtop, gtop, 0, 0), (clat - 2, bottom, dbottom, gbottom, 1, clat - 1)):
                for q in range(5):
                    src = fields.at[HALO_FIELDS[q]] if q < 3 else (frac if q == 3 else helm)
                    for k in range(lev):
                        mine[q, 2 * k:2 * k + 2, :] = src[k, row:row + 2, :]
                mine[5] = jnp.full((2 * lev, LANES), depth_ref[at_depth].astype(F32))
                u = jnp.where(lane8 < 2, turn(mine[3], 2), mine[0])
                diag[0] = jnp.where(lane8 == 2, turn(mine[4], 3), u)
                diag[1] = mine[1]
                diag[2] = mine[2]
                g = mine[0]
                for q in range(1, 5):
                    at = 11 if q == 4 else 3 * q
                    g = jnp.where(lane8 >= at, turn(mine[q], at), g)
                thin[...] = g

                @pl.when(jnp.logical_not((upper, lower)[n]))
                def _():
                    for land in ((above, la, ra), (below, lb, rb))[n]:
                        land[...] = jnp.zeros_like(land)
            @pl.when(jnp.logical_not(first | last))
            def _():
                pl.semaphore_wait(barrier, 2 + 3 * rows_beyond)

            @pl.when(second)
            def _():
                greet(ready_sem, 1, 6, 7)

            @pl.when(first)
            def _():
                pl.semaphore_wait(ready_sem, 1 + rows_beyond)

            @pl.when(jnp.logical_not(first | last))
            def _():
                westward()

            for n in range(2):
                @pl.when((upper, lower)[n])
                def _():
                    beyond[2 + n].start()

            @pl.when(jnp.logical_not(last))
            def _():
                for g in ORDER[:3]:
                    mains[g].start()

    @pl.when(first)
    def _():
        pl.semaphore_wait(barrier, 1 + 2 * rows_beyond)

    @pl.when(first | last)
    def _():
        westward()

    inside = (upper, lower)
    flat = lambda x: x.reshape(nk, LANES)
    tall3 = lambda x: x.reshape(lev, BAND, LANES)
    band_rows = [pl.ds(b * BAND, BAND) for b in range(bands)]
    ext_rows = [pl.ds((b + 1) * BAND, BAND) for b in range(bands)]
    depths = [depth_ref[b * BAND] for b in range(bands)]
    taps = (-1, 0, 1, 2)

    def tap_sum(x, depth, weights):
        total = None
        for o, w in zip(taps, weights):
            term = w * pltpu.roll(x, (depth + o + LANES) & (LANES - 1), axis=1)
            total = term if total is None else total + term
        return total

    for b in range(bands):
        weights = interp_weights(flat(frac[:, band_rows[b], :]))
        for o, w in zip(taps, weights):
            wts[o + 1, :, band_rows[b], :] = tall3(jnp.where(lane < depths[b] + o, w, 0.0))
        brink[:, band_rows[b], :] = tall3(jnp.where((lane == LANES - 1) & (depths[b] == 0), weights[0], 0.0))
        weights = [jnp.where(lane < depths[b] + o, 0.0, w) for o, w in zip(taps, weights)]
        weights[0] = jnp.where(lane < LANES - 1 + depths[b], weights[0], 0.0)
        for f in range(5):
            departed[f, :, band_rows[b], :] = tall3(tap_sum(flat(fields[f, :, band_rows[b], :]), depths[b], weights))
        hel[0, :, ext_rows[b], :] = helm[:, band_rows[b], :]

    past_edge = lane >= LANES - 2

    def east_side():
        west_copy.wait_recv()
        brim = flat(edge_i[...])
        for b in range(bands):
            shore = flat(brink[:, band_rows[b], :])
            weights = interp_weights(turn(brim, -(32 * b + 15)))
            got = [flat(departed[f, :, band_rows[b], :]) + shore * turn(brim, -(32 * b + 3 * f + 1)) for f in range(5)]
            old = [flat(ext[q, 1, :, ext_rows[b], :]) for q in range(3)]
            he = jnp.where(past_edge, flat(hel[1, :, ext_rows[b], :]), turn(brim, -(32 * b + 17)))
            past = [
                tap_sum(jnp.where(lane < 3, turn(brim, -(32 * b + 3 * f)), flat(fields[f, :, band_rows[b], :])), depths[b], weights)
                for f in HALO_FIELDS
            ]
            for f in range(5):
                departed[f, :, band_rows[b], :] = tall3(got[f])
            for q, f in enumerate(HALO_FIELDS):
                ext[q, 0, :, ext_rows[b], :] = tall3(got[f])
                ext[q, 1, :, ext_rows[b], :] = tall3(jnp.where(past_edge, old[q], past[q]))
            hel[1, :, ext_rows[b], :] = tall3(he)

    @pl.when(first)
    def _():
        east_side()

    mains[ORDER[0]].wait_recv()
    mains[ORDER[1]].wait_recv()
    rest = jnp.concatenate([turn(main_i[ORDER[1], lev + tile], SPARE - at) for tile, at in REST], axis=0)
    for b in range(bands):
        weights = [jnp.where(past_edge, w, flat(wts[o, :, band_rows[b], :]))
                   for o, w in enumerate(interp_weights(turn(rest, 18 - 3 * b)))]
        he = jnp.where(past_edge, turn(rest, 17 - 3 * b), flat(hel[1, :, ext_rows[b], :]))
        for o in range(4):
            wts[o, :, band_rows[b], :] = tall3(weights[o])
        hel[1, :, ext_rows[b], :] = tall3(he)

    def finish(f):
        tiles = [main_i[f, n] for n in range(main_i.shape[1])]
        near = [
            jnp.concatenate(
                [turn(tiles[lev + n // PER_TILE], LANES - NEAR - n % PER_TILE * NEAR)
                 for n in range(slot, len(pieces), last_slot)], axis=0)
            for slot in range(last_slot)
        ]
        near.append(jnp.concatenate(
            [jnp.where(thin_lane >= LANES - FILL, turn(tiles[k], -FILL),
                       turn(tiles[-1], LANES - NEAR - tail - (NEAR - FILL) * k)) for k in range(lev)], axis=0))
        deep = jnp.concatenate(tiles[:lev], axis=0)
        old = [flat(departed[f, :, band_rows[b], :]) for b in range(bands)]
        q = HALO_FIELDS.index(f) if f in HALO_FIELDS else None
        if q is not None:
            edge_old = [flat(ext[q, 1, :, ext_rows[b], :]) for b in range(bands)]
        more = []
        for b in range(bands):
            left = near[min(b, last_slot)]
            if 0 < b <= last_slot:
                left = jnp.where(jets < b, near[b - 1], left)
            left = jnp.where(jets == b, deep, left)
            if q is not None:
                left = jnp.where((lane == 0) & (depths[b] == 0), flat(fields[f, :, band_rows[b], :]), left)
            more.append(tap_sum(left, depths[b], [flat(wts[o, :, band_rows[b], :]) for o in range(4)]))
        for b in range(bands):
            got = old[b] + jnp.where(past_edge, 0.0, more[b])
            departed[f, :, band_rows[b], :] = tall3(got)
            if q is not None:
                ext[q, 0, :, ext_rows[b], :] = tall3(got)
                ext[q, 1, :, ext_rows[b], :] = tall3(jnp.where(past_edge, more[b], edge_old[b]))

    for f in ORDER:
        if f not in ORDER[:2]:
            mains[f].wait_recv()
        finish(f)
        if f == ORDER[2]:
            @pl.when(jnp.logical_not(first))
            def _():
                east_side()

            for n, c in enumerate(beyond):
                @pl.when((lower, upper)[n % 2])
                def _():
                    c.wait_recv()
            halo_rows(lev, clat, inside, above, below, la, lb, ra, rb, ext, hel)
            solve(lev, clat, inside, helm, ext, hel, rhs_s, p1_s, pressure)
    for n, c in enumerate(beyond):
        @pl.when((upper, lower)[n % 2])
        def _():
            c.wait_send()
    for c in (west_copy, *mains.values()):
        c.wait_send()


def halo_rows(lev, clat, inside, above, below, la, lb, ra, rb, ext, hel):
    lane = lane_of((BAND, LANES))
    stores = []
    for side, (mine, diag, thin) in enumerate(((above, la, ra), (below, lb, rb))):
        depth = jnp.max(mine[5]).astype(jnp.int32)
        own = [mine[q] for q in range(3)]
        left = [diag[q] for q in range(3)]
        g = thin[...]
        right = [turn(g, -3 * q) for q in range(3)]
        fr = jnp.where(lane < 64, turn(g, -9), turn(left[0], -2))
        he = jnp.where(lane < 64, turn(g, -11), turn(left[0], -3))
        got = depart(own, left, right, depth, interp_weights(mine[3]))
        past = depart_beside(own, left, right, depth, interp_weights(fr))
        for q in range(3):
            stores.append((side, ext.at[q, 0], jnp.where(inside[side], got[q], 0.0)))
            stores.append((side, ext.at[q, 1], jnp.where(inside[side], past[q], 0.0)))
        stores.append((side, hel.at[0], mine[4]))
        stores.append((side, hel.at[1], he))
    for side, ref, value in stores:
        at = BAND - 2 if side == 0 else BAND + clat
        for k in range(lev):
            ref[k, at:at + 2, :] = value[2 * k:2 * k + 2]


def solve(lev, clat, inside, helm, ext, hel, rhs_s, p1_s, pressure):
    tall = clat + BAND
    row = lax.broadcasted_iota(jnp.int32, (lev, tall, LANES), 1)
    outside = ((row == 0) & jnp.logical_not(inside[0])) | ((row == clat + 1) & jnp.logical_not(inside[1]))
    first = BAND - 1
    flat = lambda x: x.reshape(-1, LANES)
    mid, up, down = pl.ds(first, tall), pl.ds(first - 1, tall), pl.ds(first + 1, tall)
    u_all = beside_pair(flat(ext[0, 0, :, mid, :]), flat(ext[0, 1, :, mid, :]))
    phi = [flat(ext[2, h, :, mid, :]) for h in range(2)]
    phi_all = beside_pair(*phi)
    p1, rhs = [], []
    for h in range(2):
        div = 0.5 * (u_all[h][0] - u_all[h][1] + flat(ext[1, h, :, down, :]) - flat(ext[1, h, :, up, :]))
        rhs.append(phi[h] - 0.5 * div)
        around = phi_all[h][0] + phi_all[h][1] + flat(ext[2, h, :, down, :]) + flat(ext[2, h, :, up, :])
        p1.append((rhs[h] + around) / (4.0 + flat(hel[h, :, mid, :])))
    for h in range(2):
        p1_s[h] = jnp.where(outside, 0.0, p1[h].reshape(lev, tall, LANES))
    rhs_s[...] = rhs[0].reshape(lev, tall, LANES)
    mid = pl.ds(1, clat)
    east, west = beside_pair(flat(p1_s[0, :, mid, :]), flat(p1_s[1, :, mid, :]))[0]
    around = east + west + flat(p1_s[0, :, pl.ds(2, clat), :]) + flat(p1_s[0, :, pl.ds(0, clat), :])
    pressure[...] = ((flat(rhs_s[:, mid, :]) + around) / (4.0 + flat(helm[...]))).reshape(lev, clat, LANES)


def store(departed, pressure, departed_o, pressure_o, sem):
    copies = [pltpu.make_async_copy(departed, departed_o, sem.at[0]), pltpu.make_async_copy(pressure, pressure_o, sem.at[1])]
    for c in copies:
        c.start()
    for c in copies:
        c.wait()


def local(fields, depth, frac, helm):
    lev, clat, clon = fields.shape[1:]
    hbm = pl.BlockSpec(memory_space=pltpu.HBM)
    vmem = pl.BlockSpec(memory_space=pltpu.VMEM)
    sent = [(5, lev + REST[-1][0] + 1, BAND, clon), (lev, BAND, clon), (6, 2 * lev, clon), (6, 2 * lev, clon),
            (3, 2 * lev, clon), (3, 2 * lev, clon), (2 * lev, clon), (2 * lev, clon)]
    tall = clat + 2 * BAND
    departed, pressure = pl.pallas_call(
        functools.partial(whole_step, lev, clat),
        out_shape=[pltpu.VMEM(fields.shape, F32), pltpu.VMEM(frac.shape, F32)],
        in_specs=[hbm] * 4,
        out_specs=[vmem, vmem],
        scratch_shapes=[
            pltpu.SMEM(depth.shape, jnp.int32),
            pltpu.VMEM(fields.shape, F32), pltpu.VMEM(frac.shape, F32), pltpu.VMEM(helm.shape, F32),
            *[pltpu.VMEM(t, F32) for t in sent],
            *[pltpu.VMEM(t, F32) for t in sent],
            pltpu.VMEM((3, 2, lev, tall, clon), F32),
            pltpu.VMEM((2, lev, tall, clon), F32),
            pltpu.VMEM((lev, clat + BAND, clon), F32),
            pltpu.VMEM((2, lev, clat + BAND, clon), F32),
            pltpu.VMEM((4, *frac.shape), F32),
            pltpu.VMEM(frac.shape, F32),
            pltpu.SemaphoreType.DMA((8,)),
            pltpu.SemaphoreType.DMA((12,)),
            pltpu.SemaphoreType.DMA((12,)),
            pltpu.SemaphoreType.REGULAR,
        ],
        compiler_params=pltpu.CompilerParams(collective_id=0, has_side_effects=True, vmem_limit_bytes=24 << 20),
        name="step",
    )(*[pltpu.with_memory_space_constraint(x, pltpu.HBM) for x in (depth, fields, frac, helm)])
    return pl.pallas_call(
        store,
        out_shape=[jax.ShapeDtypeStruct(fields.shape, F32), jax.ShapeDtypeStruct(frac.shape, F32)],
        in_specs=[vmem, vmem],
        out_specs=[hbm, hbm],
        scratch_shapes=[pltpu.SemaphoreType.DMA((2,))],
        compiler_params=pltpu.CompilerParams(vmem_limit_bytes=1 << 20),
        name="store",
    )(*[pltpu.with_memory_space_constraint(x, pltpu.VMEM) for x in (departed, pressure)])


def solution(mesh):
    placed = (P(None, None, "lat", "lon"), P("lat"), P(None, "lat", "lon"), P(None, "lat", "lon"))
    return jax.shard_map(
        local,
        mesh=mesh,
        in_specs=placed,
        out_specs=(P(None, None, "lat", "lon"), P(None, "lat", "lon")),
        check_vma=False,
    )
```

```python
import functools

import jax
import jax.numpy as jnp
from jax import lax
from jax.experimental import pallas as pl
from jax.experimental.pallas import tpu as pltpu
from jax.sharding import PartitionSpec as P

BAND = 8
SHALLOW = 32
LANES = 128
NEAR = SHALLOW + 4
F32 = jnp.float32
MESH = pl.DeviceIdType.MESH
HALO_FIELDS = (0, 1, 3)
SPARE = 108
FILL = 28
CHUNK = 25
PER_TILE = 3
REST = ((0, 108), (1, 108), (2, 104), (2, 116))


def turn(x, shift):
    shift %= LANES
    return x if shift == 0 else pltpu.roll(x, shift, axis=1)


def turn_rows(x, shift):
    return pltpu.roll(x, shift % x.shape[0], axis=0)


def lane_of(shape):
    return lax.broadcasted_iota(jnp.int32, shape, len(shape) - 1)


def jet_band(depth_ref, bands):
    jet = jnp.int32(0)
    for b in range(1, bands):
        jet = jnp.where(depth_ref[b * BAND] > SHALLOW, b, jet)
    return jet


def interp_weights(frac):
    s = -frac
    below, above = (s - 1.0) * s, (s + 1.0) * (s + 2.0)
    return [
        s * above * (1.0 / 6.0),
        (s - 1.0) * above * -0.5,
        below * (s + 2.0) * 0.5,
        below * (s + 1.0) * (-1.0 / 6.0),
    ]


def depart(own, left, right, depth, weights):
    lane = lane_of(own[0].shape)
    totals = [jnp.zeros_like(own[0]) for _ in own]
    for o, w in zip((-1, 0, 1, 2), weights):
        s = depth + o
        t = lane + s
        shift = (s + LANES) & (LANES - 1)
        for n in range(len(own)):
            x = jnp.where(t <= LANES - 1, own[n], left[n])
            if o == -1:
                x = jnp.where(t == -1, right[n], x)
            totals[n] = totals[n] + w * pltpu.roll(x, shift, axis=1)
    return totals


def depart_beside(own, left, right, depth, weights):
    lane = lane_of(own[0].shape)
    totals = [jnp.zeros_like(own[0]) for _ in own]
    for o, w in zip((-1, 0, 1, 2), weights):
        s = depth + o
        t = lane + s
        shift = (s + LANES) & (LANES - 1)
        for n in range(len(own)):
            x = jnp.where(t <= LANES - 1, left[n], own[n])
            if o < 2:
                x = jnp.where((t >= 0) & (t <= 1), right[n], x)
            if o == -1:
                x = jnp.where(t == -1, own[n], x)
            totals[n] = totals[n] + w * pltpu.roll(x, shift, axis=1)
    return totals


def beside_pair(own, halo):
    lane = lane_of(own.shape)
    first, last = lane == 0, lane == LANES - 1
    return (
        (turn(jnp.where(first, halo, own), -1), turn(jnp.where(last, halo, own), 1)),
        (turn(jnp.where(first, own, halo), -1), turn(jnp.where(last, own, halo), 1)),
    )


ORDER = (0, 1, 3, 2, 4)


def whole_step(lev, clat, depth_hbm, fields_hbm, frac_hbm, helm_hbm, departed, pressure,
               depth_ref, fields, frac, helm, main, edge, top, bottom, dtop, dbottom, gtop, gbottom,
               main_i, edge_i, above, below, la, lb, ra, rb,
               ext, hel, rhs_s, p1_s, wts, brink, in_sem, send_sem, recv_sem, ready_sem):
    bands = clat // BAND
    loads = [
        pltpu.make_async_copy(src, dst, in_sem.at[i])
        for i, (src, dst) in enumerate(
            ((depth_hbm, depth_ref), (frac_hbm, frac), (helm_hbm, helm),
             *[(fields_hbm.at[f], fields.at[f]) for f in ORDER]))
    ]
    for n in (0, 3, 4, 5, 1, 2, 6, 7):
        loads[n].start()
    nlon, nlat = lax.axis_size("lon"), lax.axis_size("lat")
    i, j = lax.axis_index("lon"), lax.axis_index("lat")
    east, west = lax.rem(i + 1, nlon), lax.rem(i + nlon - 1, nlon)
    south, north = j + 1, j - 1
    upper, lower = j > 0, j < nlat - 1
    rows_beyond = upper.astype(jnp.int32) + lower.astype(jnp.int32)
    peers = [{"lon": a, "lat": b} for a, b in (
        (east, j), (west, j), (i, north), (i, south),
        (east, north), (east, south), (west, north), (west, south))]

    def greet(semaphore, side, up, down):
        pl.semaphore_signal(semaphore, inc=1, device_id=peers[side], device_id_type=MESH)
        for there, peer in ((upper, up), (lower, down)):
            @pl.when(there)
            def _():
                pl.semaphore_signal(semaphore, inc=1, device_id=peers[peer], device_id_type=MESH)

    first, last = i == 0, i == nlon - 1
    second = i == 1
    yields = last & (lax.rem(j, 2) == 1)
    barrier = pltpu.get_barrier_semaphore()
    greet(barrier, 0, 4, 5)

    @pl.when(jnp.logical_not(second))
    def _():
        greet(barrier, 1, 6, 7)

    for there, peer in ((upper, 2), (lower, 3)):
        @pl.when(there)
        def _():
            pl.semaphore_signal(barrier, inc=1, device_id=peers[peer], device_id_type=MESH)

    def copy(n, src, dst, peer):
        return pltpu.make_async_remote_copy(
            src_ref=src, dst_ref=dst, send_sem=send_sem.at[n], recv_sem=recv_sem.at[n],
            device_id=peers[peer], device_id_type=MESH)

    mains = {f: copy(7 + f, main.at[f], main_i.at[f], 0) for f in range(5)}
    west_copy = copy(0, edge, edge_i, 1)
    beyond = [
        copy(1, top, below, 2),
        copy(2, bottom, above, 3),
        copy(3, dtop, lb, 4),
        copy(4, dbottom, la, 5),
        copy(5, gtop, rb, 6),
        copy(6, gbottom, ra, 7),
    ]
    def westward():
        west_copy.start()
        for n in range(2):
            @pl.when((upper, lower)[n])
            def _():
                beyond[n].start()
                beyond[4 + n].start()

    for load in (loads[0], loads[3]):
        load.wait()
    jet = jet_band(depth_ref, bands)
    nk = lev * BAND
    lane = lane_of((nk, LANES))
    jets = jnp.full((nk, LANES), jet)
    thin_lane = lane_of((BAND, LANES))
    last_slot = bands - 2
    pieces = [(slot, k) for k in range(lev) for slot in range(last_slot)]
    tail = len(pieces) % PER_TILE * NEAR

    def level(x, k):
        return x[k * BAND:(k + 1) * BAND]

    for f in ORDER:
        if f == ORDER[1]:
            for n in (4, 1, 2):
                loads[n].wait()
            rest = None
            for b in range(bands):
                at = SPARE + 3 * b
                rows = pl.ds(b * BAND, BAND)
                fr = turn(frac[:, rows, :].reshape(nk, LANES), at - (LANES - 2))
                he = turn(helm[:, rows, :].reshape(nk, LANES), at + 2 - (LANES - 1))
                rest = fr if rest is None else jnp.where(lane >= at, fr, rest)
                rest = jnp.where(lane >= at + 2, he, rest)
        if f == ORDER[2]:
            loads[5].wait()
        x = [fields[f, :, pl.ds(b * BAND, BAND), :].reshape(nk, LANES) for b in range(bands)]
        deep = x[0]
        for b in range(1, bands):
            deep = jnp.where(jets == b, x[b], deep)
        slots = [jnp.where(jets > slot, x[slot], x[slot + 1]) for slot in range(bands - 1)]
        deep = jnp.where(lane < FILL, turn(slots[last_slot], FILL), deep)
        main[f, 0:lev] = deep.reshape(lev, BAND, LANES)
        packed = []
        for n, (slot, k) in enumerate(pieces):
            at = n % PER_TILE * NEAR
            y = turn(level(slots[slot], k), at + NEAR - LANES)
            if at == 0:
                packed.append(y)
            else:
                packed[-1] = jnp.where(thin_lane >= at, y, packed[-1])
        for k in range(lev):
            at = tail + (NEAR - FILL) * k
            packed[-1] = jnp.where(thin_lane >= at, turn(level(slots[last_slot], k), at + NEAR - LANES), packed[-1])
        if f == ORDER[1]:
            for k, (tile, at) in enumerate(REST):
                packed[tile] = jnp.where(thin_lane >= at, turn(level(rest, k), at - SPARE), packed[tile])
        for n, y in enumerate(packed):
            main[f, lev + n] = y
        if f in ORDER[3:]:
            @pl.when(jnp.logical_not(yields))
            def _():
                mains[f].start()
        else:
            @pl.when(last)
            def _():
                if f == ORDER[0]:
                    pl.semaphore_wait(barrier, 2 + 3 * rows_beyond)
                mains[f].start()

        if f == ORDER[2]:
            for n in (6, 7):
                loads[n].wait()
            acc = jnp.zeros((nk, LANES), F32)
            for b in range(bands):
                rows = pl.ds(b * BAND, BAND)
                for n in range(7):
                    src = fields[n, :, rows, :] if n < 5 else (frac if n == 5 else helm)[:, rows, :]
                    at = 32 * b + (17 if n == 6 else 3 * n)
                    acc = jnp.where(lane >= at, turn(src.reshape(nk, LANES), at), acc)
            edge[...] = acc.reshape(lev, BAND, LANES)
            lane8 = lane_of((2 * lev, LANES))
            row8 = lax.broadcasted_iota(jnp.int32, (2 * lev, LANES), 0)
            for row, mine, diag, thin, n, at_depth in (
                    (0, top, dtop, gtop, 0, 0), (clat - 2, bottom, dbottom, gbottom, 1, clat - 1)):
                taken = [
                    [src[k, row:row + 2, :] for k in range(lev)]
                    for src in (*[fields.at[f] for f in HALO_FIELDS], frac, helm)
                ]
                for q in range(5):
                    for k in range(lev):
                        mine[q, 2 * k:2 * k + 2, :] = taken[q][k]
                mine[5] = jnp.full((2 * lev, LANES), depth_ref[at_depth].astype(F32))
                whole = [mine[q] for q in range(5)]
                odd = turn_rows(whole[0], 1)
                near, far = [
                    jnp.where(row8 % 2 == n, turn(whole[0], -at), turn(odd, -at - CHUNK)) for at in (FILL, FILL + 2 * CHUNK)
                ]
                wind = jnp.where(lane8 < FILL, turn(whole[4], FILL), whole[1])
                wind = jnp.where(lane8 < FILL - 1, turn(whole[3], FILL - 1), wind)
                g = whole[0]
                for q in range(1, 5):
                    at = 11 if q == 4 else 3 * q
                    g = jnp.where(lane8 >= at, turn(whole[q], at), g)
                diag[0] = jnp.where(lane8 < CHUNK, near, wind)
                diag[1] = jnp.where(lane8 < CHUNK, far, whole[2])
                thin[...] = g

                @pl.when(jnp.logical_not((upper, lower)[n]))
                def _():
                    for land in ((above, la, ra), (below, lb, rb))[n]:
                        land[...] = jnp.zeros_like(land)
            @pl.when(jnp.logical_not(first | last))
            def _():
                pl.semaphore_wait(barrier, 2 + 3 * rows_beyond)

            @pl.when(second)
            def _():
                greet(ready_sem, 1, 6, 7)

            @pl.when(first)
            def _():
                pl.semaphore_wait(ready_sem, 1 + rows_beyond)

            @pl.when(jnp.logical_not(first | last))
            def _():
                westward()

            for n in range(2):
                @pl.when((upper, lower)[n])
                def _():
                    beyond[2 + n].start()

            @pl.when(jnp.logical_not(last))
            def _():
                for g in ORDER[:3]:
                    mains[g].start()

    @pl.when(first)
    def _():
        pl.semaphore_wait(barrier, 1 + 2 * rows_beyond)

    @pl.when(first | last)
    def _():
        westward()

    @pl.when(yields)
    def _():
        for f in ORDER[3:]:
            mains[f].start()

    inside = (upper, lower)
    flat = lambda x: x.reshape(nk, LANES)
    tall3 = lambda x: x.reshape(lev, BAND, LANES)
    band_rows = [pl.ds(b * BAND, BAND) for b in range(bands)]
    ext_rows = [pl.ds((b + 1) * BAND, BAND) for b in range(bands)]
    depths = [depth_ref[b * BAND] for b in range(bands)]
    taps = (-1, 0, 1, 2)

    def tap_sum(x, depth, weights):
        total = None
        for o, w in zip(taps, weights):
            term = w * pltpu.roll(x, (depth + o + LANES) & (LANES - 1), axis=1)
            total = term if total is None else total + term
        return total

    for b in range(bands):
        weights = interp_weights(flat(frac[:, band_rows[b], :]))
        for o, w in zip(taps, weights):
            wts[o + 1, :, band_rows[b], :] = tall3(jnp.where(lane < depths[b] + o, w, 0.0))
        brink[:, band_rows[b], :] = tall3(jnp.where((lane == LANES - 1) & (depths[b] == 0), weights[0], 0.0))
        weights = [jnp.where(lane < depths[b] + o, 0.0, w) for o, w in zip(taps, weights)]
        weights[0] = jnp.where(lane < LANES - 1 + depths[b], weights[0], 0.0)
        for f in range(5):
            departed[f, :, band_rows[b], :] = tall3(tap_sum(flat(fields[f, :, band_rows[b], :]), depths[b], weights))
        hel[0, :, ext_rows[b], :] = helm[:, band_rows[b], :]

    past_edge = lane >= LANES - 2

    def east_side():
        west_copy.wait_recv()
        brim = flat(edge_i[...])
        for b in range(bands):
            shore = flat(brink[:, band_rows[b], :])
            weights = interp_weights(turn(brim, -(32 * b + 15)))
            got = [flat(departed[f, :, band_rows[b], :]) + shore * turn(brim, -(32 * b + 3 * f + 1)) for f in range(5)]
            old = [flat(ext[q, 1, :, ext_rows[b], :]) for q in range(3)]
            he = jnp.where(past_edge, flat(hel[1, :, ext_rows[b], :]), turn(brim, -(32 * b + 17)))
            past = [
                tap_sum(jnp.where(lane < 3, turn(brim, -(32 * b + 3 * f)), flat(fields[f, :, band_rows[b], :])), depths[b], weights)
                for f in HALO_FIELDS
            ]
            for f in range(5):
                departed[f, :, band_rows[b], :] = tall3(got[f])
            for q, f in enumerate(HALO_FIELDS):
                ext[q, 0, :, ext_rows[b], :] = tall3(got[f])
                ext[q, 1, :, ext_rows[b], :] = tall3(jnp.where(past_edge, old[q], past[q]))
            hel[1, :, ext_rows[b], :] = tall3(he)

    @pl.when(first)
    def _():
        east_side()

    mains[ORDER[0]].wait_recv()
    mains[ORDER[1]].wait_recv()
    rest = jnp.concatenate([turn(main_i[ORDER[1], lev + tile], SPARE - at) for tile, at in REST], axis=0)
    for b in range(bands):
        weights = [jnp.where(past_edge, w, flat(wts[o, :, band_rows[b], :]))
                   for o, w in enumerate(interp_weights(turn(rest, 18 - 3 * b)))]
        he = jnp.where(past_edge, turn(rest, 17 - 3 * b), flat(hel[1, :, ext_rows[b], :]))
        for o in range(4):
            wts[o, :, band_rows[b], :] = tall3(weights[o])
        hel[1, :, ext_rows[b], :] = tall3(he)

    def finish(f):
        tiles = [main_i[f, n] for n in range(main_i.shape[1])]
        near = [
            jnp.concatenate(
                [turn(tiles[lev + n // PER_TILE], LANES - NEAR - n % PER_TILE * NEAR)
                 for n in range(slot, len(pieces), last_slot)], axis=0)
            for slot in range(last_slot)
        ]
        near.append(jnp.concatenate(
            [jnp.where(thin_lane >= LANES - FILL, turn(tiles[k], -FILL),
                       turn(tiles[-1], LANES - NEAR - tail - (NEAR - FILL) * k)) for k in range(lev)], axis=0))
        deep = jnp.concatenate(tiles[:lev], axis=0)
        old = [flat(departed[f, :, band_rows[b], :]) for b in range(bands)]
        q = HALO_FIELDS.index(f) if f in HALO_FIELDS else None
        if q is not None:
            edge_old = [flat(ext[q, 1, :, ext_rows[b], :]) for b in range(bands)]
        more = []
        for b in range(bands):
            left = near[min(b, last_slot)]
            if 0 < b <= last_slot:
                left = jnp.where(jets < b, near[b - 1], left)
            left = jnp.where(jets == b, deep, left)
            if q is not None:
                left = jnp.where((lane == 0) & (depths[b] == 0), flat(fields[f, :, band_rows[b], :]), left)
            more.append(tap_sum(left, depths[b], [flat(wts[o, :, band_rows[b], :]) for o in range(4)]))
        for b in range(bands):
            got = old[b] + jnp.where(past_edge, 0.0, more[b])
            departed[f, :, band_rows[b], :] = tall3(got)
            if q is not None:
                ext[q, 0, :, ext_rows[b], :] = tall3(got)
                ext[q, 1, :, ext_rows[b], :] = tall3(jnp.where(past_edge, more[b], edge_old[b]))

    for f in ORDER:
        if f not in ORDER[:2]:
            mains[f].wait_recv()
        finish(f)
        if f == ORDER[2]:
            @pl.when(jnp.logical_not(first))
            def _():
                east_side()

            for n, c in enumerate(beyond):
                @pl.when((lower, upper)[n % 2])
                def _():
                    c.wait_recv()
            halo_rows(lev, clat, inside, above, below, la, lb, ra, rb, ext, hel)
            solve(lev, clat, inside, helm, ext, hel, rhs_s, p1_s, pressure)
    for n, c in enumerate(beyond):
        @pl.when((upper, lower)[n % 2])
        def _():
            c.wait_send()
    for c in (west_copy, *mains.values()):
        c.wait_send()


def halo_rows(lev, clat, inside, above, below, la, lb, ra, rb, ext, hel):
    lane = lane_of((BAND, LANES))
    stores = []
    for side, (mine, diag, thin) in enumerate(((above, la, ra), (below, lb, rb))):
        depth = jnp.max(mine[5]).astype(jnp.int32)
        own = [mine[q] for q in range(3)]
        wind, height = diag[0], diag[1]
        u = jnp.where(lane < FILL + CHUNK, turn(wind, FILL), turn_rows(turn(wind, FILL + CHUNK), -1))
        u = jnp.where(lane < FILL + 2 * CHUNK, u, turn(height, FILL + 2 * CHUNK))
        u = jnp.where(lane < FILL + 3 * CHUNK, u, turn_rows(turn(height, FILL + 3 * CHUNK), -1))
        left = [u, wind, height]
        g = thin[...]
        right = [turn(g, -3 * q) for q in range(3)]
        fr = jnp.where(lane < 64, turn(g, -9), turn(wind, LANES - FILL + 1))
        he = jnp.where(lane < 64, turn(g, -11), turn(wind, LANES - FILL))
        got = depart(own, left, right, depth, interp_weights(mine[3]))
        past = depart_beside(own, left, right, depth, interp_weights(fr))
        for q in range(3):
            stores.append((side, ext.at[q, 0], jnp.where(inside[side], got[q], 0.0)))
            stores.append((side, ext.at[q, 1], jnp.where(inside[side], past[q], 0.0)))
        stores.append((side, hel.at[0], mine[4]))
        stores.append((side, hel.at[1], he))
    for side, ref, value in stores:
        at = BAND - 2 if side == 0 else BAND + clat
        for k in range(lev):
            ref[k, at:at + 2, :] = value[2 * k:2 * k + 2]


def solve(lev, clat, inside, helm, ext, hel, rhs_s, p1_s, pressure):
    tall = clat + BAND
    row = lax.broadcasted_iota(jnp.int32, (lev, tall, LANES), 1)
    outside = ((row == 0) & jnp.logical_not(inside[0])) | ((row == clat + 1) & jnp.logical_not(inside[1]))
    first = BAND - 1
    flat = lambda x: x.reshape(-1, LANES)
    mid, up, down = pl.ds(first, tall), pl.ds(first - 1, tall), pl.ds(first + 1, tall)
    u_all = beside_pair(flat(ext[0, 0, :, mid, :]), flat(ext[0, 1, :, mid, :]))
    phi = [flat(ext[2, h, :, mid, :]) for h in range(2)]
    phi_all = beside_pair(*phi)
    p1, rhs = [], []
    for h in range(2):
        div = 0.5 * (u_all[h][0] - u_all[h][1] + flat(ext[1, h, :, down, :]) - flat(ext[1, h, :, up, :]))
        rhs.append(phi[h] - 0.5 * div)
        around = phi_all[h][0] + phi_all[h][1] + flat(ext[2, h, :, down, :]) + flat(ext[2, h, :, up, :])
        p1.append((rhs[h] + around) / (4.0 + flat(hel[h, :, mid, :])))
    for h in range(2):
        p1_s[h] = jnp.where(outside, 0.0, p1[h].reshape(lev, tall, LANES))
    rhs_s[...] = rhs[0].reshape(lev, tall, LANES)
    mid = pl.ds(1, clat)
    east, west = beside_pair(flat(p1_s[0, :, mid, :]), flat(p1_s[1, :, mid, :]))[0]
    around = east + west + flat(p1_s[0, :, pl.ds(2, clat), :]) + flat(p1_s[0, :, pl.ds(0, clat), :])
    pressure[...] = ((flat(rhs_s[:, mid, :]) + around) / (4.0 + flat(helm[...]))).reshape(lev, clat, LANES)


def store(departed, pressure, departed_o, pressure_o, sem):
    copies = [pltpu.make_async_copy(departed, departed_o, sem.at[0]), pltpu.make_async_copy(pressure, pressure_o, sem.at[1])]
    for c in copies:
        c.start()
    for c in copies:
        c.wait()


def local(fields, depth, frac, helm):
    lev, clat, clon = fields.shape[1:]
    hbm = pl.BlockSpec(memory_space=pltpu.HBM)
    vmem = pl.BlockSpec(memory_space=pltpu.VMEM)
    sent = [(5, lev + REST[-1][0] + 1, BAND, clon), (lev, BAND, clon), (6, 2 * lev, clon), (6, 2 * lev, clon),
            (2, 2 * lev, clon), (2, 2 * lev, clon), (2 * lev, clon), (2 * lev, clon)]
    tall = clat + 2 * BAND
    departed, pressure = pl.pallas_call(
        functools.partial(whole_step, lev, clat),
        out_shape=[pltpu.VMEM(fields.shape, F32), pltpu.VMEM(frac.shape, F32)],
        in_specs=[hbm] * 4,
        out_specs=[vmem, vmem],
        scratch_shapes=[
            pltpu.SMEM(depth.shape, jnp.int32),
            pltpu.VMEM(fields.shape, F32), pltpu.VMEM(frac.shape, F32), pltpu.VMEM(helm.shape, F32),
            *[pltpu.VMEM(t, F32) for t in sent],
            *[pltpu.VMEM(t, F32) for t in sent],
            pltpu.VMEM((3, 2, lev, tall, clon), F32),
            pltpu.VMEM((2, lev, tall, clon), F32),
            pltpu.VMEM((lev, clat + BAND, clon), F32),
            pltpu.VMEM((2, lev, clat + BAND, clon), F32),
            pltpu.VMEM((4, *frac.shape), F32),
            pltpu.VMEM(frac.shape, F32),
            pltpu.SemaphoreType.DMA((8,)),
            pltpu.SemaphoreType.DMA((12,)),
            pltpu.SemaphoreType.DMA((12,)),
            pltpu.SemaphoreType.REGULAR,
        ],
        compiler_params=pltpu.CompilerParams(collective_id=0, has_side_effects=True, vmem_limit_bytes=24 << 20),
        name="step",
    )(*[pltpu.with_memory_space_constraint(x, pltpu.HBM) for x in (depth, fields, frac, helm)])
    return pl.pallas_call(
        store,
        out_shape=[jax.ShapeDtypeStruct(fields.shape, F32), jax.ShapeDtypeStruct(frac.shape, F32)],
        in_specs=[vmem, vmem],
        out_specs=[hbm, hbm],
        scratch_shapes=[pltpu.SemaphoreType.DMA((2,))],
        compiler_params=pltpu.CompilerParams(vmem_limit_bytes=1 << 20),
        name="store",
    )(*[pltpu.with_memory_space_constraint(x, pltpu.VMEM) for x in (departed, pressure)])


def solution(mesh):
    placed = (P(None, None, "lat", "lon"), P("lat"), P(None, "lat", "lon"), P(None, "lat", "lon"))
    return jax.shard_map(
        local,
        mesh=mesh,
        in_specs=placed,
        out_specs=(P(None, None, "lat", "lon"), P(None, "lat", "lon")),
        check_vma=False,
    )
```

```python
import functools

import jax
import jax.numpy as jnp
from jax import lax
from jax.experimental import pallas as pl
from jax.experimental.pallas import tpu as pltpu
from jax.sharding import PartitionSpec as P

BAND = 8
SHALLOW = 32
LANES = 128
NEAR = SHALLOW + 4
F32 = jnp.float32
MESH = pl.DeviceIdType.MESH
HALO_FIELDS = (0, 1, 3)
SPARE = 108
FILL = 28
CHUNK = 25
PER_TILE = 3
REST = ((0, 108), (1, 108), (2, 104), (2, 116))


def turn(x, shift):
    shift %= LANES
    return x if shift == 0 else pltpu.roll(x, shift, axis=1)


def turn_rows(x, shift):
    return pltpu.roll(x, shift % x.shape[0], axis=0)


def lane_of(shape):
    return lax.broadcasted_iota(jnp.int32, shape, len(shape) - 1)


def jet_band(depth_ref, bands):
    jet = jnp.int32(0)
    for b in range(1, bands):
        jet = jnp.where(depth_ref[b * BAND] > SHALLOW, b, jet)
    return jet


def interp_weights(frac):
    s = -frac
    below, above = (s - 1.0) * s, (s + 1.0) * (s + 2.0)
    return [
        s * above * (1.0 / 6.0),
        (s - 1.0) * above * -0.5,
        below * (s + 2.0) * 0.5,
        below * (s + 1.0) * (-1.0 / 6.0),
    ]


def depart(own, left, right, depth, weights):
    lane = lane_of(own[0].shape)
    totals = [jnp.zeros_like(own[0]) for _ in own]
    for o, w in zip((-1, 0, 1, 2), weights):
        s = depth + o
        t = lane + s
        shift = (s + LANES) & (LANES - 1)
        for n in range(len(own)):
            x = jnp.where(t <= LANES - 1, own[n], left[n])
            if o == -1:
                x = jnp.where(t == -1, right[n], x)
            totals[n] = totals[n] + w * pltpu.roll(x, shift, axis=1)
    return totals


def depart_beside(own, left, right, depth, weights):
    lane = lane_of(own[0].shape)
    totals = [jnp.zeros_like(own[0]) for _ in own]
    for o, w in zip((-1, 0, 1, 2), weights):
        s = depth + o
        t = lane + s
        shift = (s + LANES) & (LANES - 1)
        for n in range(len(own)):
            x = jnp.where(t <= LANES - 1, left[n], own[n])
            if o < 2:
                x = jnp.where((t >= 0) & (t <= 1), right[n], x)
            if o == -1:
                x = jnp.where(t == -1, own[n], x)
            totals[n] = totals[n] + w * pltpu.roll(x, shift, axis=1)
    return totals


def beside_pair(own, halo):
    lane = lane_of(own.shape)
    first, last = lane == 0, lane == LANES - 1
    return (
        (turn(jnp.where(first, halo, own), -1), turn(jnp.where(last, halo, own), 1)),
        (turn(jnp.where(first, own, halo), -1), turn(jnp.where(last, own, halo), 1)),
    )


ORDER = (0, 1, 3, 2, 4)


def whole_step(lev, clat, depth_hbm, fields_hbm, frac_hbm, helm_hbm, departed, pressure,
               depth_ref, fields, frac, helm, main, edge, top, bottom, dtop, dbottom, gtop, gbottom,
               main_i, edge_i, above, below, la, lb, ra, rb,
               ext, hel, rhs_s, p1_s, wts, wslot, brink, in_sem, send_sem, recv_sem, ready_sem):
    bands = clat // BAND
    loads = [
        pltpu.make_async_copy(src, dst, in_sem.at[i])
        for i, (src, dst) in enumerate(
            ((depth_hbm, depth_ref), (frac_hbm, frac), (helm_hbm, helm),
             *[(fields_hbm.at[f], fields.at[f]) for f in ORDER]))
    ]
    for n in (0, 3, 4, 5, 1, 2, 6, 7):
        loads[n].start()
    nlon, nlat = lax.axis_size("lon"), lax.axis_size("lat")
    i, j = lax.axis_index("lon"), lax.axis_index("lat")
    east, west = lax.rem(i + 1, nlon), lax.rem(i + nlon - 1, nlon)
    south, north = j + 1, j - 1
    upper, lower = j > 0, j < nlat - 1
    rows_beyond = upper.astype(jnp.int32) + lower.astype(jnp.int32)
    peers = [{"lon": a, "lat": b} for a, b in (
        (east, j), (west, j), (i, north), (i, south),
        (east, north), (east, south), (west, north), (west, south))]

    def greet(semaphore, side, up, down):
        pl.semaphore_signal(semaphore, inc=1, device_id=peers[side], device_id_type=MESH)
        for there, peer in ((upper, up), (lower, down)):
            @pl.when(there)
            def _():
                pl.semaphore_signal(semaphore, inc=1, device_id=peers[peer], device_id_type=MESH)

    first, last = i == 0, i == nlon - 1
    second = i == 1
    yields = last & (lax.rem(j, 2) == 1)
    barrier = pltpu.get_barrier_semaphore()
    greet(barrier, 0, 4, 5)

    @pl.when(jnp.logical_not(second))
    def _():
        greet(barrier, 1, 6, 7)

    for there, peer in ((upper, 2), (lower, 3)):
        @pl.when(there)
        def _():
            pl.semaphore_signal(barrier, inc=1, device_id=peers[peer], device_id_type=MESH)

    def copy(n, src, dst, peer):
        return pltpu.make_async_remote_copy(
            src_ref=src, dst_ref=dst, send_sem=send_sem.at[n], recv_sem=recv_sem.at[n],
            device_id=peers[peer], device_id_type=MESH)

    mains = {f: copy(7 + f, main.at[f], main_i.at[f], 0) for f in range(5)}
    west_copy = copy(0, edge, edge_i, 1)
    beyond = [
        copy(1, top, below, 2),
        copy(2, bottom, above, 3),
        copy(3, dtop, lb, 4),
        copy(4, dbottom, la, 5),
        copy(5, gtop, rb, 6),
        copy(6, gbottom, ra, 7),
    ]
    def westward():
        west_copy.start()
        for n in range(2):
            @pl.when((upper, lower)[n])
            def _():
                beyond[n].start()
                beyond[4 + n].start()

    for load in (loads[0], loads[3]):
        load.wait()
    jet = jet_band(depth_ref, bands)
    nk = lev * BAND
    lane = lane_of((nk, LANES))
    jets = jnp.full((nk, LANES), jet)
    thin_lane = lane_of((BAND, LANES))
    last_slot = bands - 2
    pieces = [(slot, k) for k in range(lev) for slot in range(last_slot)]
    tail = len(pieces) % PER_TILE * NEAR

    def level(x, k):
        return x[k * BAND:(k + 1) * BAND]

    for f in ORDER:
        if f == ORDER[1]:
            for n in (4, 1, 2):
                loads[n].wait()
            rest = None
            for b in range(bands):
                at = SPARE + 3 * b
                rows = pl.ds(b * BAND, BAND)
                fr = turn(frac[:, rows, :].reshape(nk, LANES), at - (LANES - 2))
                he = turn(helm[:, rows, :].reshape(nk, LANES), at + 2 - (LANES - 1))
                rest = fr if rest is None else jnp.where(lane >= at, fr, rest)
                rest = jnp.where(lane >= at + 2, he, rest)
        if f == ORDER[2]:
            loads[5].wait()
        x = [fields[f, :, pl.ds(b * BAND, BAND), :].reshape(nk, LANES) for b in range(bands)]
        deep = x[0]
        for b in range(1, bands):
            deep = jnp.where(jets == b, x[b], deep)
        slots = [jnp.where(jets > slot, x[slot], x[slot + 1]) for slot in range(bands - 1)]
        deep = jnp.where(lane < FILL, turn(slots[last_slot], FILL), deep)
        main[f, 0:lev] = deep.reshape(lev, BAND, LANES)
        packed = []
        for n, (slot, k) in enumerate(pieces):
            at = n % PER_TILE * NEAR
            y = turn(level(slots[slot], k), at + NEAR - LANES)
            if at == 0:
                packed.append(y)
            else:
                packed[-1] = jnp.where(thin_lane >= at, y, packed[-1])
        for k in range(lev):
            at = tail + (NEAR - FILL) * k
            packed[-1] = jnp.where(thin_lane >= at, turn(level(slots[last_slot], k), at + NEAR - LANES), packed[-1])
        if f == ORDER[1]:
            for k, (tile, at) in enumerate(REST):
                packed[tile] = jnp.where(thin_lane >= at, turn(level(rest, k), at - SPARE), packed[tile])
        for n, y in enumerate(packed):
            main[f, lev + n] = y
        if f in ORDER[3:]:
            @pl.when(jnp.logical_not(yields))
            def _():
                mains[f].start()
        else:
            @pl.when(last)
            def _():
                if f == ORDER[0]:
                    pl.semaphore_wait(barrier, 2 + 3 * rows_beyond)
                mains[f].start()

        if f == ORDER[2]:
            for n in (6, 7):
                loads[n].wait()
            acc = jnp.zeros((nk, LANES), F32)
            for b in range(bands):
                rows = pl.ds(b * BAND, BAND)
                for n in range(7):
                    src = fields[n, :, rows, :] if n < 5 else (frac if n == 5 else helm)[:, rows, :]
                    at = 32 * b + (17 if n == 6 else 3 * n)
                    acc = jnp.where(lane >= at, turn(src.reshape(nk, LANES), at), acc)
            edge[...] = acc.reshape(lev, BAND, LANES)
            lane8 = lane_of((2 * lev, LANES))
            row8 = lax.broadcasted_iota(jnp.int32, (2 * lev, LANES), 0)
            for row, mine, diag, thin, n, at_depth in (
                    (0, top, dtop, gtop, 0, 0), (clat - 2, bottom, dbottom, gbottom, 1, clat - 1)):
                taken = [
                    [src[k, row:row + 2, :] for k in range(lev)]
                    for src in (*[fields.at[f] for f in HALO_FIELDS], frac, helm)
                ]
                for q in range(5):
                    for k in range(lev):
                        mine[q, 2 * k:2 * k + 2, :] = taken[q][k]
                mine[5] = jnp.full((2 * lev, LANES), depth_ref[at_depth].astype(F32))
                whole = [mine[q] for q in range(5)]
                odd = turn_rows(whole[0], 1)
                near, far = [
                    jnp.where(row8 % 2 == n, turn(whole[0], -at), turn(odd, -at - CHUNK)) for at in (FILL, FILL + 2 * CHUNK)
                ]
                wind = jnp.where(lane8 < FILL, turn(whole[4], FILL), whole[1])
                wind = jnp.where(lane8 < FILL - 1, turn(whole[3], FILL - 1), wind)
                g = whole[0]
                for q in range(1, 5):
                    at = 11 if q == 4 else 3 * q
                    g = jnp.where(lane8 >= at, turn(whole[q], at), g)
                diag[0] = jnp.where(lane8 < CHUNK, near, wind)
                diag[1] = jnp.where(lane8 < CHUNK, far, whole[2])
                thin[...] = g

                @pl.when(jnp.logical_not((upper, lower)[n]))
                def _():
                    for land in ((above, la, ra), (below, lb, rb))[n]:
                        land[...] = jnp.zeros_like(land)
            @pl.when(jnp.logical_not(first | last))
            def _():
                pl.semaphore_wait(barrier, 2 + 3 * rows_beyond)

            @pl.when(second)
            def _():
                greet(ready_sem, 1, 6, 7)

            @pl.when(first)
            def _():
                pl.semaphore_wait(ready_sem, 1 + rows_beyond)

            @pl.when(jnp.logical_not(first | last))
            def _():
                westward()

            for n in range(2):
                @pl.when((upper, lower)[n])
                def _():
                    beyond[2 + n].start()

            @pl.when(jnp.logical_not(last))
            def _():
                for g in ORDER[:3]:
                    mains[g].start()

    @pl.when(first)
    def _():
        pl.semaphore_wait(barrier, 1 + 2 * rows_beyond)

    @pl.when(first | last)
    def _():
        westward()

    @pl.when(yields)
    def _():
        for f in ORDER[3:]:
            mains[f].start()

    inside = (upper, lower)
    flat = lambda x: x.reshape(nk, LANES)
    tall3 = lambda x: x.reshape(lev, BAND, LANES)
    band_rows = [pl.ds(b * BAND, BAND) for b in range(bands)]
    ext_rows = [pl.ds((b + 1) * BAND, BAND) for b in range(bands)]
    depths = [depth_ref[b * BAND] for b in range(bands)]
    taps = (-1, 0, 1, 2)

    def tap_sum(x, depth, weights):
        total = None
        for o, w in zip(taps, weights):
            term = w * pltpu.roll(x, (depth + o + LANES) & (LANES - 1), axis=1)
            total = term if total is None else total + term
        return total

    for b in range(bands):
        weights = interp_weights(flat(frac[:, band_rows[b], :]))
        for o, w in zip(taps, weights):
            wts[o + 1, :, band_rows[b], :] = tall3(jnp.where(lane < depths[b] + o, w, 0.0))
        brink[:, band_rows[b], :] = tall3(jnp.where((lane == LANES - 1) & (depths[b] == 0), weights[0], 0.0))
        weights = [jnp.where(lane < depths[b] + o, 0.0, w) for o, w in zip(taps, weights)]
        weights[0] = jnp.where(lane < LANES - 1 + depths[b], weights[0], 0.0)
        for f in range(5):
            departed[f, :, band_rows[b], :] = tall3(tap_sum(flat(fields[f, :, band_rows[b], :]), depths[b], weights))
        hel[0, :, ext_rows[b], :] = helm[:, band_rows[b], :]

    past_edge = lane >= LANES - 2

    def east_side():
        west_copy.wait_recv()
        brim = flat(edge_i[...])
        for b in range(bands):
            shore = flat(brink[:, band_rows[b], :])
            weights = interp_weights(turn(brim, -(32 * b + 15)))
            got = [flat(departed[f, :, band_rows[b], :]) + shore * turn(brim, -(32 * b + 3 * f + 1)) for f in range(5)]
            old = [flat(ext[q, 1, :, ext_rows[b], :]) for q in range(3)]
            he = jnp.where(past_edge, flat(hel[1, :, ext_rows[b], :]), turn(brim, -(32 * b + 17)))
            past = [
                tap_sum(jnp.where(lane < 3, turn(brim, -(32 * b + 3 * f)), flat(fields[f, :, band_rows[b], :])), depths[b], weights)
                for f in HALO_FIELDS
            ]
            for f in range(5):
                departed[f, :, band_rows[b], :] = tall3(got[f])
            for q, f in enumerate(HALO_FIELDS):
                ext[q, 0, :, ext_rows[b], :] = tall3(got[f])
                ext[q, 1, :, ext_rows[b], :] = tall3(jnp.where(past_edge, old[q], past[q]))
            hel[1, :, ext_rows[b], :] = tall3(he)

    @pl.when(first)
    def _():
        east_side()

    slot_depths = [jnp.where(jet > slot, depths[slot], depths[slot + 1]) for slot in range(bands - 1)]
    jet_depth = depths[0]
    for b in range(1, bands):
        jet_depth = jnp.where(jet == b, depths[b], jet_depth)
    for o in range(4):
        by_band = [flat(wts[o, :, band_rows[b], :]) for b in range(bands)]
        whole = by_band[0]
        for b in range(1, bands):
            whole = jnp.where(jets == b, by_band[b], whole)
        for slot in range(bands - 1):
            wslot[o, :, band_rows[slot], :] = tall3(jnp.where(jets > slot, by_band[slot], by_band[slot + 1]))
        wslot[o, :, band_rows[bands - 1], :] = tall3(whole)

    def finish_whole(f):
        tiles = [main_i[f, n] for n in range(main_i.shape[1])]
        old = [flat(departed[f, :, band_rows[b], :]) for b in range(bands)]

        def shifted(x, amount):
            return pltpu.roll(x, (amount + 2 * LANES) & (LANES - 1), axis=1)

        sums = [[] for _ in range(bands)]
        for k in range(lev):
            for slot in range(bands):
                depth = jet_depth if slot == bands - 1 else slot_depths[slot]
                total = None
                for n, o in enumerate(taps):
                    if slot == bands - 1:
                        x = shifted(tiles[k], depth + o)
                    elif slot == last_slot:
                        x = jnp.where(
                            thin_lane < depth + o - FILL,
                            shifted(tiles[-1], depth + o + LANES - NEAR - tail - (NEAR - FILL) * k),
                            shifted(tiles[k], depth + o - FILL))
                    else:
                        at = k * last_slot + slot
                        x = shifted(tiles[lev + at // PER_TILE], depth + o - NEAR - at % PER_TILE * NEAR)
                    term = wslot[n, k, band_rows[slot], :] * x
                    total = term if total is None else total + term
                sums[slot].append(total)
        sums = [jnp.concatenate(x, axis=0) for x in sums]
        for b in range(bands):
            more = sums[min(b, last_slot)]
            if 0 < b <= last_slot:
                more = jnp.where(jets < b, sums[b - 1], more)
            more = jnp.where(jets == b, sums[bands - 1], more)
            departed[f, :, band_rows[b], :] = tall3(old[b] + more)

    mains[ORDER[0]].wait_recv()
    mains[ORDER[1]].wait_recv()
    rest = jnp.concatenate([turn(main_i[ORDER[1], lev + tile], SPARE - at) for tile, at in REST], axis=0)
    for b in range(bands):
        weights = [jnp.where(past_edge, w, flat(wts[o, :, band_rows[b], :]))
                   for o, w in enumerate(interp_weights(turn(rest, 18 - 3 * b)))]
        he = jnp.where(past_edge, turn(rest, 17 - 3 * b), flat(hel[1, :, ext_rows[b], :]))
        for o in range(4):
            wts[o, :, band_rows[b], :] = tall3(weights[o])
        hel[1, :, ext_rows[b], :] = tall3(he)

    def finish(f):
        tiles = [main_i[f, n] for n in range(main_i.shape[1])]
        near = [
            jnp.concatenate(
                [turn(tiles[lev + n // PER_TILE], LANES - NEAR - n % PER_TILE * NEAR)
                 for n in range(slot, len(pieces), last_slot)], axis=0)
            for slot in range(last_slot)
        ]
        near.append(jnp.concatenate(
            [jnp.where(thin_lane >= LANES - FILL, turn(tiles[k], -FILL),
                       turn(tiles[-1], LANES - NEAR - tail - (NEAR - FILL) * k)) for k in range(lev)], axis=0))
        deep = jnp.concatenate(tiles[:lev], axis=0)
        old = [flat(departed[f, :, band_rows[b], :]) for b in range(bands)]
        q = HALO_FIELDS.index(f) if f in HALO_FIELDS else None
        if q is not None:
            edge_old = [flat(ext[q, 1, :, ext_rows[b], :]) for b in range(bands)]
        more = []
        for b in range(bands):
            left = near[min(b, last_slot)]
            if 0 < b <= last_slot:
                left = jnp.where(jets < b, near[b - 1], left)
            left = jnp.where(jets == b, deep, left)
            if q is not None:
                left = jnp.where((lane == 0) & (depths[b] == 0), flat(fields[f, :, band_rows[b], :]), left)
            more.append(tap_sum(left, depths[b], [flat(wts[o, :, band_rows[b], :]) for o in range(4)]))
        for b in range(bands):
            got = old[b] + jnp.where(past_edge, 0.0, more[b])
            departed[f, :, band_rows[b], :] = tall3(got)
            if q is not None:
                ext[q, 0, :, ext_rows[b], :] = tall3(got)
                ext[q, 1, :, ext_rows[b], :] = tall3(jnp.where(past_edge, more[b], edge_old[b]))

    for f in ORDER:
        if f not in ORDER[:2]:
            mains[f].wait_recv()
        if f in HALO_FIELDS:
            finish(f)
        else:
            finish_whole(f)
        if f == ORDER[2]:
            @pl.when(jnp.logical_not(first))
            def _():
                east_side()

            for n, c in enumerate(beyond):
                @pl.when((lower, upper)[n % 2])
                def _():
                    c.wait_recv()
            halo_rows(lev, clat, inside, above, below, la, lb, ra, rb, ext, hel)
            solve(lev, clat, inside, helm, ext, hel, rhs_s, p1_s, pressure)
    for n, c in enumerate(beyond):
        @pl.when((upper, lower)[n % 2])
        def _():
            c.wait_send()
    for c in (west_copy, *mains.values()):
        c.wait_send()


def halo_rows(lev, clat, inside, above, below, la, lb, ra, rb, ext, hel):
    lane = lane_of((BAND, LANES))
    stores = []
    for side, (mine, diag, thin) in enumerate(((above, la, ra), (below, lb, rb))):
        depth = jnp.max(mine[5]).astype(jnp.int32)
        own = [mine[q] for q in range(3)]
        wind, height = diag[0], diag[1]
        u = jnp.where(lane < FILL + CHUNK, turn(wind, FILL), turn_rows(turn(wind, FILL + CHUNK), -1))
        u = jnp.where(lane < FILL + 2 * CHUNK, u, turn(height, FILL + 2 * CHUNK))
        u = jnp.where(lane < FILL + 3 * CHUNK, u, turn_rows(turn(height, FILL + 3 * CHUNK), -1))
        left = [u, wind, height]
        g = thin[...]
        right = [turn(g, -3 * q) for q in range(3)]
        fr = jnp.where(lane < 64, turn(g, -9), turn(wind, LANES - FILL + 1))
        he = jnp.where(lane < 64, turn(g, -11), turn(wind, LANES - FILL))
        got = depart(own, left, right, depth, interp_weights(mine[3]))
        past = depart_beside(own, left, right, depth, interp_weights(fr))
        for q in range(3):
            stores.append((side, ext.at[q, 0], jnp.where(inside[side], got[q], 0.0)))
            stores.append((side, ext.at[q, 1], jnp.where(inside[side], past[q], 0.0)))
        stores.append((side, hel.at[0], mine[4]))
        stores.append((side, hel.at[1], he))
    for side, ref, value in stores:
        at = BAND - 2 if side == 0 else BAND + clat
        for k in range(lev):
            ref[k, at:at + 2, :] = value[2 * k:2 * k + 2]


def solve(lev, clat, inside, helm, ext, hel, rhs_s, p1_s, pressure):
    tall = clat + BAND
    row = lax.broadcasted_iota(jnp.int32, (lev, tall, LANES), 1)
    outside = ((row == 0) & jnp.logical_not(inside[0])) | ((row == clat + 1) & jnp.logical_not(inside[1]))
    first = BAND - 1
    flat = lambda x: x.reshape(-1, LANES)
    mid, up, down = pl.ds(first, tall), pl.ds(first - 1, tall), pl.ds(first + 1, tall)
    u_all = beside_pair(flat(ext[0, 0, :, mid, :]), flat(ext[0, 1, :, mid, :]))
    phi = [flat(ext[2, h, :, mid, :]) for h in range(2)]
    phi_all = beside_pair(*phi)
    p1, rhs = [], []
    for h in range(2):
        div = 0.5 * (u_all[h][0] - u_all[h][1] + flat(ext[1, h, :, down, :]) - flat(ext[1, h, :, up, :]))
        rhs.append(phi[h] - 0.5 * div)
        around = phi_all[h][0] + phi_all[h][1] + flat(ext[2, h, :, down, :]) + flat(ext[2, h, :, up, :])
        p1.append((rhs[h] + around) / (4.0 + flat(hel[h, :, mid, :])))
    for h in range(2):
        p1_s[h] = jnp.where(outside, 0.0, p1[h].reshape(lev, tall, LANES))
    rhs_s[...] = rhs[0].reshape(lev, tall, LANES)
    mid = pl.ds(1, clat)
    east, west = beside_pair(flat(p1_s[0, :, mid, :]), flat(p1_s[1, :, mid, :]))[0]
    around = east + west + flat(p1_s[0, :, pl.ds(2, clat), :]) + flat(p1_s[0, :, pl.ds(0, clat), :])
    pressure[...] = ((flat(rhs_s[:, mid, :]) + around) / (4.0 + flat(helm[...]))).reshape(lev, clat, LANES)


def store(departed, pressure, departed_o, pressure_o, sem):
    copies = [pltpu.make_async_copy(departed, departed_o, sem.at[0]), pltpu.make_async_copy(pressure, pressure_o, sem.at[1])]
    for c in copies:
        c.start()
    for c in copies:
        c.wait()


def local(fields, depth, frac, helm):
    lev, clat, clon = fields.shape[1:]
    hbm = pl.BlockSpec(memory_space=pltpu.HBM)
    vmem = pl.BlockSpec(memory_space=pltpu.VMEM)
    sent = [(5, lev + REST[-1][0] + 1, BAND, clon), (lev, BAND, clon), (6, 2 * lev, clon), (6, 2 * lev, clon),
            (2, 2 * lev, clon), (2, 2 * lev, clon), (2 * lev, clon), (2 * lev, clon)]
    tall = clat + 2 * BAND
    departed, pressure = pl.pallas_call(
        functools.partial(whole_step, lev, clat),
        out_shape=[pltpu.VMEM(fields.shape, F32), pltpu.VMEM(frac.shape, F32)],
        in_specs=[hbm] * 4,
        out_specs=[vmem, vmem],
        scratch_shapes=[
            pltpu.SMEM(depth.shape, jnp.int32),
            pltpu.VMEM(fields.shape, F32), pltpu.VMEM(frac.shape, F32), pltpu.VMEM(helm.shape, F32),
            *[pltpu.VMEM(t, F32) for t in sent],
            *[pltpu.VMEM(t, F32) for t in sent],
            pltpu.VMEM((3, 2, lev, tall, clon), F32),
            pltpu.VMEM((2, lev, tall, clon), F32),
            pltpu.VMEM((lev, clat + BAND, clon), F32),
            pltpu.VMEM((2, lev, clat + BAND, clon), F32),
            pltpu.VMEM((4, *frac.shape), F32),
            pltpu.VMEM((4, *frac.shape), F32),
            pltpu.VMEM(frac.shape, F32),
            pltpu.SemaphoreType.DMA((8,)),
            pltpu.SemaphoreType.DMA((12,)),
            pltpu.SemaphoreType.DMA((12,)),
            pltpu.SemaphoreType.REGULAR,
        ],
        compiler_params=pltpu.CompilerParams(collective_id=0, has_side_effects=True, vmem_limit_bytes=24 << 20),
        name="step",
    )(*[pltpu.with_memory_space_constraint(x, pltpu.HBM) for x in (depth, fields, frac, helm)])
    return pl.pallas_call(
        store,
        out_shape=[jax.ShapeDtypeStruct(fields.shape, F32), jax.ShapeDtypeStruct(frac.shape, F32)],
        in_specs=[vmem, vmem],
        out_specs=[hbm, hbm],
        scratch_shapes=[pltpu.SemaphoreType.DMA((2,))],
        compiler_params=pltpu.CompilerParams(vmem_limit_bytes=1 << 20),
        name="store",
    )(*[pltpu.with_memory_space_constraint(x, pltpu.VMEM) for x in (departed, pressure)])


def solution(mesh):
    placed = (P(None, None, "lat", "lon"), P("lat"), P(None, "lat", "lon"), P(None, "lat", "lon"))
    return jax.shard_map(
        local,
        mesh=mesh,
        in_specs=placed,
        out_specs=(P(None, None, "lat", "lon"), P(None, "lat", "lon")),
        check_vma=False,
    )
```

```python
import functools

import jax
import jax.numpy as jnp
from jax import lax
from jax.experimental import pallas as pl
from jax.experimental.pallas import tpu as pltpu
from jax.sharding import PartitionSpec as P

BAND = 8
SHALLOW = 32
LANES = 128
NEAR = SHALLOW + 4
F32 = jnp.float32
MESH = pl.DeviceIdType.MESH
HALO_FIELDS = (0, 1, 3)
SPARE = 108
FILL = 28
CHUNK = 25
PER_TILE = 3
REST = ((0, 108), (1, 108), (2, 104), (2, 116))


def turn(x, shift):
    shift %= LANES
    return x if shift == 0 else pltpu.roll(x, shift, axis=1)


def turn_rows(x, shift):
    return pltpu.roll(x, shift % x.shape[0], axis=0)


def lane_of(shape):
    return lax.broadcasted_iota(jnp.int32, shape, len(shape) - 1)


def jet_band(depth_ref, bands):
    jet = jnp.int32(0)
    for b in range(1, bands):
        jet = jnp.where(depth_ref[b * BAND] > SHALLOW, b, jet)
    return jet


def interp_weights(frac):
    s = -frac
    below, above = (s - 1.0) * s, (s + 1.0) * (s + 2.0)
    return [
        s * above * (1.0 / 6.0),
        (s - 1.0) * above * -0.5,
        below * (s + 2.0) * 0.5,
        below * (s + 1.0) * (-1.0 / 6.0),
    ]


def depart(own, left, right, depth, weights):
    lane = lane_of(own[0].shape)
    totals = [jnp.zeros_like(own[0]) for _ in own]
    for o, w in zip((-1, 0, 1, 2), weights):
        s = depth + o
        t = lane + s
        shift = (s + LANES) & (LANES - 1)
        for n in range(len(own)):
            x = jnp.where(t <= LANES - 1, own[n], left[n])
            if o == -1:
                x = jnp.where(t == -1, right[n], x)
            totals[n] = totals[n] + w * pltpu.roll(x, shift, axis=1)
    return totals


def depart_beside(own, left, right, depth, weights):
    lane = lane_of(own[0].shape)
    totals = [jnp.zeros_like(own[0]) for _ in own]
    for o, w in zip((-1, 0, 1, 2), weights):
        s = depth + o
        t = lane + s
        shift = (s + LANES) & (LANES - 1)
        for n in range(len(own)):
            x = jnp.where(t <= LANES - 1, left[n], own[n])
            if o < 2:
                x = jnp.where((t >= 0) & (t <= 1), right[n], x)
            if o == -1:
                x = jnp.where(t == -1, own[n], x)
            totals[n] = totals[n] + w * pltpu.roll(x, shift, axis=1)
    return totals


def beside_pair(own, halo):
    lane = lane_of(own.shape)
    first, last = lane == 0, lane == LANES - 1
    return (
        (turn(jnp.where(first, halo, own), -1), turn(jnp.where(last, halo, own), 1)),
        (turn(jnp.where(first, own, halo), -1), turn(jnp.where(last, own, halo), 1)),
    )


ORDER = (0, 1, 3, 2, 4)


def whole_step(lev, clat, depth_hbm, fields_hbm, frac_hbm, helm_hbm, departed, pressure,
               depth_ref, fields, frac, helm, main, edge, top, bottom, dtop, dbottom, gtop, gbottom,
               main_i, edge_i, above, below, la, lb, ra, rb,
               ext, hel, rhs_s, p1_s, wts, wslot, brink, in_sem, send_sem, recv_sem, ready_sem):
    bands = clat // BAND
    loads = [
        pltpu.make_async_copy(src, dst, in_sem.at[i])
        for i, (src, dst) in enumerate(
            ((depth_hbm, depth_ref), (frac_hbm, frac), (helm_hbm, helm),
             *[(fields_hbm.at[f], fields.at[f]) for f in ORDER]))
    ]
    for n in (3, 0):
        loads[n].start()
    nlon, nlat = lax.axis_size("lon"), lax.axis_size("lat")
    i, j = lax.axis_index("lon"), lax.axis_index("lat")
    east, west = lax.rem(i + 1, nlon), lax.rem(i + nlon - 1, nlon)
    south, north = j + 1, j - 1
    upper, lower = j > 0, j < nlat - 1
    rows_beyond = upper.astype(jnp.int32) + lower.astype(jnp.int32)
    peers = [{"lon": a, "lat": b} for a, b in (
        (east, j), (west, j), (i, north), (i, south),
        (east, north), (east, south), (west, north), (west, south))]

    def greet(semaphore, side, up, down):
        pl.semaphore_signal(semaphore, inc=1, device_id=peers[side], device_id_type=MESH)
        for there, peer in ((upper, up), (lower, down)):
            @pl.when(there)
            def _():
                pl.semaphore_signal(semaphore, inc=1, device_id=peers[peer], device_id_type=MESH)

    first, last = i == 0, i == nlon - 1
    second = i == 1
    yields = last & (lax.rem(j, 2) == 1)
    barrier = pltpu.get_barrier_semaphore()
    greet(barrier, 0, 4, 5)

    @pl.when(jnp.logical_not(second))
    def _():
        greet(barrier, 1, 6, 7)

    for there, peer in ((upper, 2), (lower, 3)):
        @pl.when(there)
        def _():
            pl.semaphore_signal(barrier, inc=1, device_id=peers[peer], device_id_type=MESH)

    for n in (4, 5, 1, 2, 6, 7):
        loads[n].start()

    def copy(n, src, dst, peer):
        return pltpu.make_async_remote_copy(
            src_ref=src, dst_ref=dst, send_sem=send_sem.at[n], recv_sem=recv_sem.at[n],
            device_id=peers[peer], device_id_type=MESH)

    mains = {f: copy(7 + f, main.at[f], main_i.at[f], 0) for f in range(5)}
    west_copy = copy(0, edge, edge_i, 1)
    beyond = [
        copy(1, top, below, 2),
        copy(2, bottom, above, 3),
        copy(3, dtop, lb, 4),
        copy(4, dbottom, la, 5),
        copy(5, gtop, rb, 6),
        copy(6, gbottom, ra, 7),
    ]
    def westward():
        west_copy.start()
        for n in range(2):
            @pl.when((upper, lower)[n])
            def _():
                beyond[n].start()
                beyond[4 + n].start()

    for load in (loads[0], loads[3]):
        load.wait()
    jet = jet_band(depth_ref, bands)
    nk = lev * BAND
    lane = lane_of((nk, LANES))
    jets = jnp.full((nk, LANES), jet)
    thin_lane = lane_of((BAND, LANES))
    last_slot = bands - 2
    pieces = [(slot, k) for k in range(lev) for slot in range(last_slot)]
    tail = len(pieces) % PER_TILE * NEAR

    def level(x, k):
        return x[k * BAND:(k + 1) * BAND]

    for f in ORDER:
        if f == ORDER[1]:
            for n in (4, 1, 2):
                loads[n].wait()
            rest = None
            for b in range(bands):
                at = SPARE + 3 * b
                rows = pl.ds(b * BAND, BAND)
                fr = turn(frac[:, rows, :].reshape(nk, LANES), at - (LANES - 2))
                he = turn(helm[:, rows, :].reshape(nk, LANES), at + 2 - (LANES - 1))
                rest = fr if rest is None else jnp.where(lane >= at, fr, rest)
                rest = jnp.where(lane >= at + 2, he, rest)
        if f == ORDER[2]:
            loads[5].wait()
        x = [fields[f, :, pl.ds(b * BAND, BAND), :].reshape(nk, LANES) for b in range(bands)]
        deep = x[0]
        for b in range(1, bands):
            deep = jnp.where(jets == b, x[b], deep)
        slots = [jnp.where(jets > slot, x[slot], x[slot + 1]) for slot in range(bands - 1)]
        deep = jnp.where(lane < FILL, turn(slots[last_slot], FILL), deep)
        main[f, 0:lev] = deep.reshape(lev, BAND, LANES)
        packed = []
        for n, (slot, k) in enumerate(pieces):
            at = n % PER_TILE * NEAR
            y = turn(level(slots[slot], k), at + NEAR - LANES)
            if at == 0:
                packed.append(y)
            else:
                packed[-1] = jnp.where(thin_lane >= at, y, packed[-1])
        for k in range(lev):
            at = tail + (NEAR - FILL) * k
            packed[-1] = jnp.where(thin_lane >= at, turn(level(slots[last_slot], k), at + NEAR - LANES), packed[-1])
        if f == ORDER[1]:
            for k, (tile, at) in enumerate(REST):
                packed[tile] = jnp.where(thin_lane >= at, turn(level(rest, k), at - SPARE), packed[tile])
        for n, y in enumerate(packed):
            main[f, lev + n] = y
        if f in ORDER[3:]:
            @pl.when(jnp.logical_not(yields))
            def _():
                mains[f].start()
        else:
            @pl.when(last)
            def _():
                if f == ORDER[0]:
                    pl.semaphore_wait(barrier, 2 + 3 * rows_beyond)
                mains[f].start()

        if f == ORDER[2]:
            for n in (6, 7):
                loads[n].wait()
            acc = jnp.zeros((nk, LANES), F32)
            for b in range(bands):
                rows = pl.ds(b * BAND, BAND)
                for n in range(7):
                    src = fields[n, :, rows, :] if n < 5 else (frac if n == 5 else helm)[:, rows, :]
                    at = 32 * b + (17 if n == 6 else 3 * n)
                    acc = jnp.where(lane >= at, turn(src.reshape(nk, LANES), at), acc)
            edge[...] = acc.reshape(lev, BAND, LANES)
            lane8 = lane_of((2 * lev, LANES))
            row8 = lax.broadcasted_iota(jnp.int32, (2 * lev, LANES), 0)
            for row, mine, diag, thin, n, at_depth in (
                    (0, top, dtop, gtop, 0, 0), (clat - 2, bottom, dbottom, gbottom, 1, clat - 1)):
                taken = [
                    [src[k, row:row + 2, :] for k in range(lev)]
                    for src in (*[fields.at[f] for f in HALO_FIELDS], frac, helm)
                ]
                for q in range(5):
                    for k in range(lev):
                        mine[q, 2 * k:2 * k + 2, :] = taken[q][k]
                mine[5] = jnp.full((2 * lev, LANES), depth_ref[at_depth].astype(F32))
                whole = [mine[q] for q in range(5)]
                odd = turn_rows(whole[0], 1)
                near, far = [
                    jnp.where(row8 % 2 == n, turn(whole[0], -at), turn(odd, -at - CHUNK)) for at in (FILL, FILL + 2 * CHUNK)
                ]
                wind = jnp.where(lane8 < FILL, turn(whole[4], FILL), whole[1])
                wind = jnp.where(lane8 < FILL - 1, turn(whole[3], FILL - 1), wind)
                g = whole[0]
                for q in range(1, 5):
                    at = 11 if q == 4 else 3 * q
                    g = jnp.where(lane8 >= at, turn(whole[q], at), g)
                diag[0] = jnp.where(lane8 < CHUNK, near, wind)
                diag[1] = jnp.where(lane8 < CHUNK, far, whole[2])
                thin[...] = g

                @pl.when(jnp.logical_not((upper, lower)[n]))
                def _():
                    for land in ((above, la, ra), (below, lb, rb))[n]:
                        land[...] = jnp.zeros_like(land)
            @pl.when(jnp.logical_not(first | last))
            def _():
                pl.semaphore_wait(barrier, 2 + 3 * rows_beyond)

            @pl.when(second)
            def _():
                greet(ready_sem, 1, 6, 7)

            @pl.when(first)
            def _():
                pl.semaphore_wait(ready_sem, 1 + rows_beyond)

            @pl.when(jnp.logical_not(first | last))
            def _():
                westward()

            for n in range(2):
                @pl.when((upper, lower)[n])
                def _():
                    beyond[2 + n].start()

            @pl.when(jnp.logical_not(last))
            def _():
                for g in ORDER[:3]:
                    mains[g].start()

    @pl.when(first)
    def _():
        pl.semaphore_wait(barrier, 1 + 2 * rows_beyond)

    @pl.when(first | last)
    def _():
        westward()

    @pl.when(yields)
    def _():
        for f in ORDER[3:]:
            mains[f].start()

    inside = (upper, lower)
    flat = lambda x: x.reshape(nk, LANES)
    tall3 = lambda x: x.reshape(lev, BAND, LANES)
    band_rows = [pl.ds(b * BAND, BAND) for b in range(bands)]
    ext_rows = [pl.ds((b + 1) * BAND, BAND) for b in range(bands)]
    depths = [depth_ref[b * BAND] for b in range(bands)]
    taps = (-1, 0, 1, 2)

    def tap_sum(x, depth, weights):
        total = None
        for o, w in zip(taps, weights):
            term = w * pltpu.roll(x, (depth + o + LANES) & (LANES - 1), axis=1)
            total = term if total is None else total + term
        return total

    for b in range(bands):
        weights = interp_weights(flat(frac[:, band_rows[b], :]))
        for o, w in zip(taps, weights):
            wts[o + 1, :, band_rows[b], :] = tall3(jnp.where(lane < depths[b] + o, w, 0.0))
        brink[:, band_rows[b], :] = tall3(jnp.where((lane == LANES - 1) & (depths[b] == 0), weights[0], 0.0))
        weights = [jnp.where(lane < depths[b] + o, 0.0, w) for o, w in zip(taps, weights)]
        weights[0] = jnp.where(lane < LANES - 1 + depths[b], weights[0], 0.0)
        for f in range(5):
            departed[f, :, band_rows[b], :] = tall3(tap_sum(flat(fields[f, :, band_rows[b], :]), depths[b], weights))
        hel[0, :, ext_rows[b], :] = helm[:, band_rows[b], :]

    past_edge = lane >= LANES - 2

    def east_side():
        west_copy.wait_recv()
        brim = flat(edge_i[...])
        for b in range(bands):
            shore = flat(brink[:, band_rows[b], :])
            weights = interp_weights(turn(brim, -(32 * b + 15)))
            got = [flat(departed[f, :, band_rows[b], :]) + shore * turn(brim, -(32 * b + 3 * f + 1)) for f in range(5)]
            old = [flat(ext[q, 1, :, ext_rows[b], :]) for q in range(3)]
            he = jnp.where(past_edge, flat(hel[1, :, ext_rows[b], :]), turn(brim, -(32 * b + 17)))
            past = [
                tap_sum(jnp.where(lane < 3, turn(brim, -(32 * b + 3 * f)), flat(fields[f, :, band_rows[b], :])), depths[b], weights)
                for f in HALO_FIELDS
            ]
            for f in range(5):
                departed[f, :, band_rows[b], :] = tall3(got[f])
            for q, f in enumerate(HALO_FIELDS):
                ext[q, 0, :, ext_rows[b], :] = tall3(got[f])
                ext[q, 1, :, ext_rows[b], :] = tall3(jnp.where(past_edge, old[q], past[q]))
            hel[1, :, ext_rows[b], :] = tall3(he)

    @pl.when(first)
    def _():
        east_side()

    slot_depths = [jnp.where(jet > slot, depths[slot], depths[slot + 1]) for slot in range(bands - 1)]
    jet_depth = depths[0]
    for b in range(1, bands):
        jet_depth = jnp.where(jet == b, depths[b], jet_depth)
    for o in range(4):
        by_band = [flat(wts[o, :, band_rows[b], :]) for b in range(bands)]
        whole = by_band[0]
        for b in range(1, bands):
            whole = jnp.where(jets == b, by_band[b], whole)
        for slot in range(bands - 1):
            wslot[o, :, band_rows[slot], :] = tall3(jnp.where(jets > slot, by_band[slot], by_band[slot + 1]))
        wslot[o, :, band_rows[bands - 1], :] = tall3(whole)

    def finish_whole(f):
        tiles = [main_i[f, n] for n in range(main_i.shape[1])]
        old = [flat(departed[f, :, band_rows[b], :]) for b in range(bands)]

        def shifted(x, amount):
            return pltpu.roll(x, (amount + 2 * LANES) & (LANES - 1), axis=1)

        sums = [[] for _ in range(bands)]
        for k in range(lev):
            for slot in range(bands):
                depth = jet_depth if slot == bands - 1 else slot_depths[slot]
                total = None
                for n, o in enumerate(taps):
                    if slot == bands - 1:
                        x = shifted(tiles[k], depth + o)
                    elif slot == last_slot:
                        x = jnp.where(
                            thin_lane < depth + o - FILL,
                            shifted(tiles[-1], depth + o + LANES - NEAR - tail - (NEAR - FILL) * k),
                            shifted(tiles[k], depth + o - FILL))
                    else:
                        at = k * last_slot + slot
                        x = shifted(tiles[lev + at // PER_TILE], depth + o - NEAR - at % PER_TILE * NEAR)
                    term = wslot[n, k, band_rows[slot], :] * x
                    total = term if total is None else total + term
                sums[slot].append(total)
        sums = [jnp.concatenate(x, axis=0) for x in sums]
        for b in range(bands):
            more = sums[min(b, last_slot)]
            if 0 < b <= last_slot:
                more = jnp.where(jets < b, sums[b - 1], more)
            more = jnp.where(jets == b, sums[bands - 1], more)
            departed[f, :, band_rows[b], :] = tall3(old[b] + more)

    mains[ORDER[0]].wait_recv()
    mains[ORDER[1]].wait_recv()
    rest = jnp.concatenate([turn(main_i[ORDER[1], lev + tile], SPARE - at) for tile, at in REST], axis=0)
    for b in range(bands):
        weights = [jnp.where(past_edge, w, flat(wts[o, :, band_rows[b], :]))
                   for o, w in enumerate(interp_weights(turn(rest, 18 - 3 * b)))]
        he = jnp.where(past_edge, turn(rest, 17 - 3 * b), flat(hel[1, :, ext_rows[b], :]))
        for o in range(4):
            wts[o, :, band_rows[b], :] = tall3(weights[o])
        hel[1, :, ext_rows[b], :] = tall3(he)

    def finish(f):
        tiles = [main_i[f, n] for n in range(main_i.shape[1])]
        near = [
            jnp.concatenate(
                [turn(tiles[lev + n // PER_TILE], LANES - NEAR - n % PER_TILE * NEAR)
                 for n in range(slot, len(pieces), last_slot)], axis=0)
            for slot in range(last_slot)
        ]
        near.append(jnp.concatenate(
            [jnp.where(thin_lane >= LANES - FILL, turn(tiles[k], -FILL),
                       turn(tiles[-1], LANES - NEAR - tail - (NEAR - FILL) * k)) for k in range(lev)], axis=0))
        deep = jnp.concatenate(tiles[:lev], axis=0)
        old = [flat(departed[f, :, band_rows[b], :]) for b in range(bands)]
        q = HALO_FIELDS.index(f) if f in HALO_FIELDS else None
        if q is not None:
            edge_old = [flat(ext[q, 1, :, ext_rows[b], :]) for b in range(bands)]
        more = []
        for b in range(bands):
            left = near[min(b, last_slot)]
            if 0 < b <= last_slot:
                left = jnp.where(jets < b, near[b - 1], left)
            left = jnp.where(jets == b, deep, left)
            if q is not None:
                left = jnp.where((lane == 0) & (depths[b] == 0), flat(fields[f, :, band_rows[b], :]), left)
            more.append(tap_sum(left, depths[b], [flat(wts[o, :, band_rows[b], :]) for o in range(4)]))
        for b in range(bands):
            got = old[b] + jnp.where(past_edge, 0.0, more[b])
            departed[f, :, band_rows[b], :] = tall3(got)
            if q is not None:
                ext[q, 0, :, ext_rows[b], :] = tall3(got)
                ext[q, 1, :, ext_rows[b], :] = tall3(jnp.where(past_edge, more[b], edge_old[b]))

    for f in ORDER:
        if f not in ORDER[:2]:
            mains[f].wait_recv()
        if f in HALO_FIELDS:
            finish(f)
        else:
            finish_whole(f)
        if f == ORDER[2]:
            @pl.when(jnp.logical_not(first))
            def _():
                east_side()

            for n, c in enumerate(beyond):
                @pl.when((lower, upper)[n % 2])
                def _():
                    c.wait_recv()
            halo_rows(lev, clat, inside, above, below, la, lb, ra, rb, ext, hel)
            solve(lev, clat, inside, helm, ext, hel, rhs_s, p1_s, pressure)
    for n, c in enumerate(beyond):
        @pl.when((upper, lower)[n % 2])
        def _():
            c.wait_send()
    for c in (west_copy, *mains.values()):
        c.wait_send()


def halo_rows(lev, clat, inside, above, below, la, lb, ra, rb, ext, hel):
    lane = lane_of((BAND, LANES))
    stores = []
    for side, (mine, diag, thin) in enumerate(((above, la, ra), (below, lb, rb))):
        depth = jnp.max(mine[5]).astype(jnp.int32)
        own = [mine[q] for q in range(3)]
        wind, height = diag[0], diag[1]
        u = jnp.where(lane < FILL + CHUNK, turn(wind, FILL), turn_rows(turn(wind, FILL + CHUNK), -1))
        u = jnp.where(lane < FILL + 2 * CHUNK, u, turn(height, FILL + 2 * CHUNK))
        u = jnp.where(lane < FILL + 3 * CHUNK, u, turn_rows(turn(height, FILL + 3 * CHUNK), -1))
        left = [u, wind, height]
        g = thin[...]
        right = [turn(g, -3 * q) for q in range(3)]
        fr = jnp.where(lane < 64, turn(g, -9), turn(wind, LANES - FILL + 1))
        he = jnp.where(lane < 64, turn(g, -11), turn(wind, LANES - FILL))
        got = depart(own, left, right, depth, interp_weights(mine[3]))
        past = depart_beside(own, left, right, depth, interp_weights(fr))
        for q in range(3):
            stores.append((side, ext.at[q, 0], jnp.where(inside[side], got[q], 0.0)))
            stores.append((side, ext.at[q, 1], jnp.where(inside[side], past[q], 0.0)))
        stores.append((side, hel.at[0], mine[4]))
        stores.append((side, hel.at[1], he))
    for side, ref, value in stores:
        at = BAND - 2 if side == 0 else BAND + clat
        for k in range(lev):
            ref[k, at:at + 2, :] = value[2 * k:2 * k + 2]


def solve(lev, clat, inside, helm, ext, hel, rhs_s, p1_s, pressure):
    tall = clat + BAND
    row = lax.broadcasted_iota(jnp.int32, (lev, tall, LANES), 1)
    outside = ((row == 0) & jnp.logical_not(inside[0])) | ((row == clat + 1) & jnp.logical_not(inside[1]))
    first = BAND - 1
    flat = lambda x: x.reshape(-1, LANES)
    mid, up, down = pl.ds(first, tall), pl.ds(first - 1, tall), pl.ds(first + 1, tall)
    u_all = beside_pair(flat(ext[0, 0, :, mid, :]), flat(ext[0, 1, :, mid, :]))
    phi = [flat(ext[2, h, :, mid, :]) for h in range(2)]
    phi_all = beside_pair(*phi)
    p1, rhs = [], []
    for h in range(2):
        div = 0.5 * (u_all[h][0] - u_all[h][1] + flat(ext[1, h, :, down, :]) - flat(ext[1, h, :, up, :]))
        rhs.append(phi[h] - 0.5 * div)
        around = phi_all[h][0] + phi_all[h][1] + flat(ext[2, h, :, down, :]) + flat(ext[2, h, :, up, :])
        p1.append((rhs[h] + around) / (4.0 + flat(hel[h, :, mid, :])))
    for h in range(2):
        p1_s[h] = jnp.where(outside, 0.0, p1[h].reshape(lev, tall, LANES))
    rhs_s[...] = rhs[0].reshape(lev, tall, LANES)
    mid = pl.ds(1, clat)
    east, west = beside_pair(flat(p1_s[0, :, mid, :]), flat(p1_s[1, :, mid, :]))[0]
    around = east + west + flat(p1_s[0, :, pl.ds(2, clat), :]) + flat(p1_s[0, :, pl.ds(0, clat), :])
    pressure[...] = ((flat(rhs_s[:, mid, :]) + around) / (4.0 + flat(helm[...]))).reshape(lev, clat, LANES)


def store(departed, pressure, departed_o, pressure_o, sem):
    copies = [pltpu.make_async_copy(departed, departed_o, sem.at[0]), pltpu.make_async_copy(pressure, pressure_o, sem.at[1])]
    for c in copies:
        c.start()
    for c in copies:
        c.wait()


def local(fields, depth, frac, helm):
    lev, clat, clon = fields.shape[1:]
    hbm = pl.BlockSpec(memory_space=pltpu.HBM)
    vmem = pl.BlockSpec(memory_space=pltpu.VMEM)
    sent = [(5, lev + REST[-1][0] + 1, BAND, clon), (lev, BAND, clon), (6, 2 * lev, clon), (6, 2 * lev, clon),
            (2, 2 * lev, clon), (2, 2 * lev, clon), (2 * lev, clon), (2 * lev, clon)]
    tall = clat + 2 * BAND
    departed, pressure = pl.pallas_call(
        functools.partial(whole_step, lev, clat),
        out_shape=[pltpu.VMEM(fields.shape, F32), pltpu.VMEM(frac.shape, F32)],
        in_specs=[hbm] * 4,
        out_specs=[vmem, vmem],
        scratch_shapes=[
            pltpu.SMEM(depth.shape, jnp.int32),
            pltpu.VMEM(fields.shape, F32), pltpu.VMEM(frac.shape, F32), pltpu.VMEM(helm.shape, F32),
            *[pltpu.VMEM(t, F32) for t in sent],
            *[pltpu.VMEM(t, F32) for t in sent],
            pltpu.VMEM((3, 2, lev, tall, clon), F32),
            pltpu.VMEM((2, lev, tall, clon), F32),
            pltpu.VMEM((lev, clat + BAND, clon), F32),
            pltpu.VMEM((2, lev, clat + BAND, clon), F32),
            pltpu.VMEM((4, *frac.shape), F32),
            pltpu.VMEM((4, *frac.shape), F32),
            pltpu.VMEM(frac.shape, F32),
            pltpu.SemaphoreType.DMA((8,)),
            pltpu.SemaphoreType.DMA((12,)),
            pltpu.SemaphoreType.DMA((12,)),
            pltpu.SemaphoreType.REGULAR,
        ],
        compiler_params=pltpu.CompilerParams(collective_id=0, has_side_effects=True, vmem_limit_bytes=24 << 20),
        name="step",
    )(*[pltpu.with_memory_space_constraint(x, pltpu.HBM) for x in (depth, fields, frac, helm)])
    return pl.pallas_call(
        store,
        out_shape=[jax.ShapeDtypeStruct(fields.shape, F32), jax.ShapeDtypeStruct(frac.shape, F32)],
        in_specs=[vmem, vmem],
        out_specs=[hbm, hbm],
        scratch_shapes=[pltpu.SemaphoreType.DMA((2,))],
        compiler_params=pltpu.CompilerParams(vmem_limit_bytes=1 << 20),
        name="store",
    )(*[pltpu.with_memory_space_constraint(x, pltpu.VMEM) for x in (departed, pressure)])


def solution(mesh):
    placed = (P(None, None, "lat", "lon"), P("lat"), P(None, "lat", "lon"), P(None, "lat", "lon"))
    return jax.shard_map(
        local,
        mesh=mesh,
        in_specs=placed,
        out_specs=(P(None, None, "lat", "lon"), P(None, "lat", "lon")),
        check_vma=False,
    )
```

```python
import functools

import jax
import jax.numpy as jnp
from jax import lax
from jax.experimental import pallas as pl
from jax.experimental.pallas import tpu as pltpu
from jax.sharding import PartitionSpec as P

BAND = 8
SHALLOW = 32
LANES = 128
NEAR = SHALLOW + 4
F32 = jnp.float32
MESH = pl.DeviceIdType.MESH
HALO_FIELDS = (0, 1, 3)
SPARE = 108
FILL = 28
CHUNK = 25
PER_TILE = 3
REST = ((0, 108), (1, 108), (2, 104), (2, 116))


def turn(x, shift):
    shift %= LANES
    return x if shift == 0 else pltpu.roll(x, shift, axis=1)


def turn_rows(x, shift):
    return pltpu.roll(x, shift % x.shape[0], axis=0)


def lane_of(shape):
    return lax.broadcasted_iota(jnp.int32, shape, len(shape) - 1)


def jet_band(depth_ref, bands):
    jet = jnp.int32(0)
    for b in range(1, bands):
        jet = jnp.where(depth_ref[b * BAND] > SHALLOW, b, jet)
    return jet


def interp_weights(frac):
    s = -frac
    below, above = (s - 1.0) * s, (s + 1.0) * (s + 2.0)
    return [
        s * above * (1.0 / 6.0),
        (s - 1.0) * above * -0.5,
        below * (s + 2.0) * 0.5,
        below * (s + 1.0) * (-1.0 / 6.0),
    ]


def depart(own, left, right, depth, weights):
    lane = lane_of(own[0].shape)
    totals = [jnp.zeros_like(own[0]) for _ in own]
    for o, w in zip((-1, 0, 1, 2), weights):
        s = depth + o
        t = lane + s
        shift = (s + LANES) & (LANES - 1)
        for n in range(len(own)):
            x = jnp.where(t <= LANES - 1, own[n], left[n])
            if o == -1:
                x = jnp.where(t == -1, right[n], x)
            totals[n] = totals[n] + w * pltpu.roll(x, shift, axis=1)
    return totals


def depart_beside(own, left, right, depth, weights):
    lane = lane_of(own[0].shape)
    totals = [jnp.zeros_like(own[0]) for _ in own]
    for o, w in zip((-1, 0, 1, 2), weights):
        s = depth + o
        t = lane + s
        shift = (s + LANES) & (LANES - 1)
        for n in range(len(own)):
            x = jnp.where(t <= LANES - 1, left[n], own[n])
            if o < 2:
                x = jnp.where((t >= 0) & (t <= 1), right[n], x)
            if o == -1:
                x = jnp.where(t == -1, own[n], x)
            totals[n] = totals[n] + w * pltpu.roll(x, shift, axis=1)
    return totals


def beside_pair(own, halo):
    lane = lane_of(own.shape)
    first, last = lane == 0, lane == LANES - 1
    return (
        (turn(jnp.where(first, halo, own), -1), turn(jnp.where(last, halo, own), 1)),
        (turn(jnp.where(first, own, halo), -1), turn(jnp.where(last, own, halo), 1)),
    )


ORDER = (0, 1, 3, 2, 4)


def whole_step(lev, clat, depth_hbm, fields_hbm, frac_hbm, helm_hbm, departed, pressure,
               depth_ref, fields, frac, helm, main, edge, top, bottom, dtop, dbottom, gtop, gbottom,
               main_i, edge_i, above, below, la, lb, ra, rb,
               ext, hel, rhs_s, p1_s, wts, wslot, brink, in_sem, send_sem, recv_sem, ready_sem):
    bands = clat // BAND
    loads = [
        pltpu.make_async_copy(src, dst, in_sem.at[i])
        for i, (src, dst) in enumerate(
            ((depth_hbm, depth_ref), (frac_hbm, frac), (helm_hbm, helm),
             *[(fields_hbm.at[f], fields.at[f]) for f in ORDER]))
    ]
    for n in (3, 0):
        loads[n].start()
    nlon, nlat = lax.axis_size("lon"), lax.axis_size("lat")
    i, j = lax.axis_index("lon"), lax.axis_index("lat")
    east, west = lax.rem(i + 1, nlon), lax.rem(i + nlon - 1, nlon)
    south, north = j + 1, j - 1
    upper, lower = j > 0, j < nlat - 1
    rows_beyond = upper.astype(jnp.int32) + lower.astype(jnp.int32)
    peers = [{"lon": a, "lat": b} for a, b in (
        (east, j), (west, j), (i, north), (i, south),
        (east, north), (east, south), (west, north), (west, south))]

    def greet(semaphore, side, up, down):
        pl.semaphore_signal(semaphore, inc=1, device_id=peers[side], device_id_type=MESH)
        for there, peer in ((upper, up), (lower, down)):
            @pl.when(there)
            def _():
                pl.semaphore_signal(semaphore, inc=1, device_id=peers[peer], device_id_type=MESH)

    first, last = i == 0, i == nlon - 1
    second = i == 1
    yields = last & (lax.rem(j, 2) == 1)
    barrier = pltpu.get_barrier_semaphore()
    greet(barrier, 0, 4, 5)

    @pl.when(jnp.logical_not(second))
    def _():
        greet(barrier, 1, 6, 7)

    for there, peer in ((upper, 2), (lower, 3)):
        @pl.when(there)
        def _():
            pl.semaphore_signal(barrier, inc=1, device_id=peers[peer], device_id_type=MESH)

    for n in (4, 5, 1, 2, 6, 7):
        loads[n].start()

    def copy(n, src, dst, peer):
        return pltpu.make_async_remote_copy(
            src_ref=src, dst_ref=dst, send_sem=send_sem.at[n], recv_sem=recv_sem.at[n],
            device_id=peers[peer], device_id_type=MESH)

    mains = {f: copy(7 + f, main.at[f], main_i.at[f], 0) for f in range(5)}
    west_copy = copy(0, edge, edge_i, 1)
    beyond = [
        copy(1, top, below, 2),
        copy(2, bottom, above, 3),
        copy(3, dtop, lb, 4),
        copy(4, dbottom, la, 5),
        copy(5, gtop, rb, 6),
        copy(6, gbottom, ra, 7),
    ]
    def westward():
        west_copy.start()
        for n in range(2):
            @pl.when((upper, lower)[n])
            def _():
                beyond[n].start()
                beyond[4 + n].start()

    for load in (loads[0], loads[3]):
        load.wait()
    jet = jet_band(depth_ref, bands)
    nk = lev * BAND
    lane = lane_of((nk, LANES))
    jets = jnp.full((nk, LANES), jet)
    thin_lane = lane_of((BAND, LANES))
    last_slot = bands - 2
    pieces = [(slot, k) for k in range(lev) for slot in range(last_slot)]
    tail = len(pieces) % PER_TILE * NEAR

    def level(x, k):
        return x[k * BAND:(k + 1) * BAND]

    for f in ORDER:
        if f == ORDER[1]:
            for n in (4, 1, 2):
                loads[n].wait()
            rest = None
            for b in range(bands):
                at = SPARE + 3 * b
                rows = pl.ds(b * BAND, BAND)
                fr = turn(frac[:, rows, :].reshape(nk, LANES), at - (LANES - 2))
                he = turn(helm[:, rows, :].reshape(nk, LANES), at + 2 - (LANES - 1))
                rest = fr if rest is None else jnp.where(lane >= at, fr, rest)
                rest = jnp.where(lane >= at + 2, he, rest)
        if f == ORDER[2]:
            loads[5].wait()
        x = [fields[f, :, pl.ds(b * BAND, BAND), :].reshape(nk, LANES) for b in range(bands)]
        deep = x[0]
        for b in range(1, bands):
            deep = jnp.where(jets == b, x[b], deep)
        slots = [jnp.where(jets > slot, x[slot], x[slot + 1]) for slot in range(bands - 1)]
        deep = jnp.where(lane < FILL, turn(slots[last_slot], FILL), deep)
        main[f, 0:lev] = deep.reshape(lev, BAND, LANES)
        packed = []
        for n, (slot, k) in enumerate(pieces):
            at = n % PER_TILE * NEAR
            y = turn(level(slots[slot], k), at + NEAR - LANES)
            if at == 0:
                packed.append(y)
            else:
                packed[-1] = jnp.where(thin_lane >= at, y, packed[-1])
        for k in range(lev):
            at = tail + (NEAR - FILL) * k
            packed[-1] = jnp.where(thin_lane >= at, turn(level(slots[last_slot], k), at + NEAR - LANES), packed[-1])
        if f == ORDER[1]:
            for k, (tile, at) in enumerate(REST):
                packed[tile] = jnp.where(thin_lane >= at, turn(level(rest, k), at - SPARE), packed[tile])
        for n, y in enumerate(packed):
            main[f, lev + n] = y
        if f in ORDER[3:]:
            @pl.when(jnp.logical_not(yields))
            def _():
                mains[f].start()
        else:
            @pl.when(last)
            def _():
                if f == ORDER[0]:
                    pl.semaphore_wait(barrier, 2 + 3 * rows_beyond)
                mains[f].start()

        if f == ORDER[2]:
            for n in (6, 7):
                loads[n].wait()
            acc = jnp.zeros((nk, LANES), F32)
            for b in range(bands):
                rows = pl.ds(b * BAND, BAND)
                for n in range(7):
                    src = fields[n, :, rows, :] if n < 5 else (frac if n == 5 else helm)[:, rows, :]
                    at = 32 * b + (17 if n == 6 else 3 * n)
                    acc = jnp.where(lane >= at, turn(src.reshape(nk, LANES), at), acc)
            edge[...] = acc.reshape(lev, BAND, LANES)
            lane8 = lane_of((2 * lev, LANES))
            row8 = lax.broadcasted_iota(jnp.int32, (2 * lev, LANES), 0)
            for row, mine, diag, thin, n, at_depth in (
                    (0, top, dtop, gtop, 0, 0), (clat - 2, bottom, dbottom, gbottom, 1, clat - 1)):
                taken = [
                    [src[k, row:row + 2, :] for k in range(lev)]
                    for src in (*[fields.at[f] for f in HALO_FIELDS], frac, helm)
                ]
                for q in range(5):
                    for k in range(lev):
                        mine[q, 2 * k:2 * k + 2, :] = taken[q][k]
                mine[5] = jnp.full((2 * lev, LANES), depth_ref[at_depth].astype(F32))
                whole = [mine[q] for q in range(5)]
                odd = turn_rows(whole[0], 1)
                near, far = [
                    jnp.where(row8 % 2 == n, turn(whole[0], -at), turn(odd, -at - CHUNK)) for at in (FILL, FILL + 2 * CHUNK)
                ]
                wind = jnp.where(lane8 < FILL, turn(whole[4], FILL), whole[1])
                wind = jnp.where(lane8 < FILL - 1, turn(whole[3], FILL - 1), wind)
                g = whole[0]
                for q in range(1, 5):
                    at = 11 if q == 4 else 3 * q
                    g = jnp.where(lane8 >= at, turn(whole[q], at), g)
                diag[0] = jnp.where(lane8 < CHUNK, near, wind)
                diag[1] = jnp.where(lane8 < CHUNK, far, whole[2])
                thin[...] = g

                @pl.when(jnp.logical_not((upper, lower)[n]))
                def _():
                    for land in ((above, la, ra), (below, lb, rb))[n]:
                        land[...] = jnp.zeros_like(land)
            @pl.when(jnp.logical_not(first | last))
            def _():
                pl.semaphore_wait(barrier, 2 + 3 * rows_beyond)

            @pl.when(second)
            def _():
                greet(ready_sem, 1, 6, 7)

            @pl.when(first)
            def _():
                pl.semaphore_wait(ready_sem, 1 + rows_beyond)

            @pl.when(jnp.logical_not(first | last))
            def _():
                westward()

            for n in range(2):
                @pl.when((upper, lower)[n])
                def _():
                    beyond[2 + n].start()

            @pl.when(jnp.logical_not(last))
            def _():
                for g in ORDER[:3]:
                    mains[g].start()

    @pl.when(first)
    def _():
        pl.semaphore_wait(barrier, 1 + 2 * rows_beyond)

    @pl.when(first | last)
    def _():
        westward()

    @pl.when(yields)
    def _():
        for f in ORDER[3:]:
            mains[f].start()

    inside = (upper, lower)
    flat = lambda x: x.reshape(nk, LANES)
    tall3 = lambda x: x.reshape(lev, BAND, LANES)
    band_rows = [pl.ds(b * BAND, BAND) for b in range(bands)]
    ext_rows = [pl.ds((b + 1) * BAND, BAND) for b in range(bands)]
    depths = [depth_ref[b * BAND] for b in range(bands)]
    taps = (-1, 0, 1, 2)

    def tap_sum(x, depth, weights):
        total = None
        for o, w in zip(taps, weights):
            term = w * pltpu.roll(x, (depth + o + LANES) & (LANES - 1), axis=1)
            total = term if total is None else total + term
        return total

    for b in range(bands):
        weights = interp_weights(flat(frac[:, band_rows[b], :]))
        for o, w in zip(taps, weights):
            wts[o + 1, :, band_rows[b], :] = tall3(jnp.where(lane < depths[b] + o, w, 0.0))
        brink[:, band_rows[b], :] = tall3(jnp.where((lane == LANES - 1) & (depths[b] == 0), weights[0], 0.0))
        weights = [jnp.where(lane < depths[b] + o, 0.0, w) for o, w in zip(taps, weights)]
        weights[0] = jnp.where(lane < LANES - 1 + depths[b], weights[0], 0.0)
        for f in range(5):
            departed[f, :, band_rows[b], :] = tall3(tap_sum(flat(fields[f, :, band_rows[b], :]), depths[b], weights))
        hel[0, :, ext_rows[b], :] = helm[:, band_rows[b], :]

    past_edge = lane >= LANES - 2

    def east_side():
        west_copy.wait_recv()
        brim = flat(edge_i[...])
        for b in range(bands):
            shore = flat(brink[:, band_rows[b], :])
            weights = interp_weights(turn(brim, -(32 * b + 15)))
            got = [flat(departed[f, :, band_rows[b], :]) + shore * turn(brim, -(32 * b + 3 * f + 1)) for f in range(5)]
            old = [flat(ext[q, 1, :, ext_rows[b], :]) for q in range(3)]
            he = jnp.where(past_edge, flat(hel[1, :, ext_rows[b], :]), turn(brim, -(32 * b + 17)))
            past = [
                tap_sum(jnp.where(lane < 3, turn(brim, -(32 * b + 3 * f)), flat(fields[f, :, band_rows[b], :])), depths[b], weights)
                for f in HALO_FIELDS
            ]
            for f in range(5):
                departed[f, :, band_rows[b], :] = tall3(got[f])
            for q, f in enumerate(HALO_FIELDS):
                ext[q, 0, :, ext_rows[b], :] = tall3(got[f])
                ext[q, 1, :, ext_rows[b], :] = tall3(jnp.where(past_edge, old[q], past[q]))
            hel[1, :, ext_rows[b], :] = tall3(he)

    @pl.when(first)
    def _():
        east_side()

    slot_depths = [jnp.where(jet > slot, depths[slot], depths[slot + 1]) for slot in range(bands - 1)]
    jet_depth = depths[0]
    for b in range(1, bands):
        jet_depth = jnp.where(jet == b, depths[b], jet_depth)
    for o in range(4):
        by_band = [flat(wts[o, :, band_rows[b], :]) for b in range(bands)]
        whole = by_band[0]
        for b in range(1, bands):
            whole = jnp.where(jets == b, by_band[b], whole)
        for slot in range(bands - 1):
            wslot[o, :, band_rows[slot], :] = tall3(jnp.where(jets > slot, by_band[slot], by_band[slot + 1]))
        wslot[o, :, band_rows[bands - 1], :] = tall3(whole)

    def finish_whole(f):
        tiles = [main_i[f, n] for n in range(main_i.shape[1])]
        old = [flat(departed[f, :, band_rows[b], :]) for b in range(bands)]

        def shifted(x, amount):
            return pltpu.roll(x, (amount + 2 * LANES) & (LANES - 1), axis=1)

        sums = [[] for _ in range(bands)]
        for k in range(lev):
            for slot in range(bands):
                depth = jet_depth if slot == bands - 1 else slot_depths[slot]
                total = None
                for n, o in enumerate(taps):
                    if slot == bands - 1:
                        x = shifted(tiles[k], depth + o)
                    elif slot == last_slot:
                        x = jnp.where(
                            thin_lane < depth + o - FILL,
                            shifted(tiles[-1], depth + o + LANES - NEAR - tail - (NEAR - FILL) * k),
                            shifted(tiles[k], depth + o - FILL))
                    else:
                        at = k * last_slot + slot
                        x = shifted(tiles[lev + at // PER_TILE], depth + o - NEAR - at % PER_TILE * NEAR)
                    term = wslot[n, k, band_rows[slot], :] * x
                    total = term if total is None else total + term
                sums[slot].append(total)
        sums = [jnp.concatenate(x, axis=0) for x in sums]
        for b in range(bands):
            more = sums[min(b, last_slot)]
            if 0 < b <= last_slot:
                more = jnp.where(jets < b, sums[b - 1], more)
            more = jnp.where(jets == b, sums[bands - 1], more)
            departed[f, :, band_rows[b], :] = tall3(old[b] + more)

    mains[ORDER[0]].wait_recv()
    mains[ORDER[1]].wait_recv()
    rest = jnp.concatenate([turn(main_i[ORDER[1], lev + tile], SPARE - at) for tile, at in REST], axis=0)
    for b in range(bands):
        weights = [jnp.where(past_edge, w, flat(wts[o, :, band_rows[b], :]))
                   for o, w in enumerate(interp_weights(turn(rest, 18 - 3 * b)))]
        he = jnp.where(past_edge, turn(rest, 17 - 3 * b), flat(hel[1, :, ext_rows[b], :]))
        for o in range(4):
            wts[o, :, band_rows[b], :] = tall3(weights[o])
        hel[1, :, ext_rows[b], :] = tall3(he)

    def finish(f):
        tiles = [main_i[f, n] for n in range(main_i.shape[1])]
        near = [
            jnp.concatenate(
                [turn(tiles[lev + n // PER_TILE], LANES - NEAR - n % PER_TILE * NEAR)
                 for n in range(slot, len(pieces), last_slot)], axis=0)
            for slot in range(last_slot)
        ]
        near.append(jnp.concatenate(
            [jnp.where(thin_lane >= LANES - FILL, turn(tiles[k], -FILL),
                       turn(tiles[-1], LANES - NEAR - tail - (NEAR - FILL) * k)) for k in range(lev)], axis=0))
        deep = jnp.concatenate(tiles[:lev], axis=0)
        old = [flat(departed[f, :, band_rows[b], :]) for b in range(bands)]
        q = HALO_FIELDS.index(f) if f in HALO_FIELDS else None
        if q is not None:
            edge_old = [flat(ext[q, 1, :, ext_rows[b], :]) for b in range(bands)]
        more = []
        for b in range(bands):
            left = near[min(b, last_slot)]
            if 0 < b <= last_slot:
                left = jnp.where(jets < b, near[b - 1], left)
            left = jnp.where(jets == b, deep, left)
            if q is not None:
                left = jnp.where((lane == 0) & (depths[b] == 0), flat(fields[f, :, band_rows[b], :]), left)
            more.append(tap_sum(left, depths[b], [flat(wts[o, :, band_rows[b], :]) for o in range(4)]))
        for b in range(bands):
            got = old[b] + jnp.where(past_edge, 0.0, more[b])
            departed[f, :, band_rows[b], :] = tall3(got)
            if q is not None:
                ext[q, 0, :, ext_rows[b], :] = tall3(got)
                ext[q, 1, :, ext_rows[b], :] = tall3(jnp.where(past_edge, more[b], edge_old[b]))

    for f in ORDER:
        if f == ORDER[4]:
            for n, c in enumerate(beyond):
                @pl.when((upper, lower)[n % 2])
                def _():
                    c.wait_send()
            for c in (west_copy, *mains.values()):
                c.wait_send()
        if f not in ORDER[:2]:
            mains[f].wait_recv()
        if f in HALO_FIELDS:
            finish(f)
        else:
            finish_whole(f)
        if f == ORDER[2]:
            @pl.when(jnp.logical_not(first))
            def _():
                east_side()

            for n, c in enumerate(beyond):
                @pl.when((lower, upper)[n % 2])
                def _():
                    c.wait_recv()
            halo_rows(lev, clat, inside, above, below, la, lb, ra, rb, ext, hel)
            solve(lev, clat, inside, helm, ext, hel, rhs_s, p1_s, pressure)


def halo_rows(lev, clat, inside, above, below, la, lb, ra, rb, ext, hel):
    lane = lane_of((BAND, LANES))
    stores = []
    for side, (mine, diag, thin) in enumerate(((above, la, ra), (below, lb, rb))):
        depth = jnp.max(mine[5]).astype(jnp.int32)
        own = [mine[q] for q in range(3)]
        wind, height = diag[0], diag[1]
        u = jnp.where(lane < FILL + CHUNK, turn(wind, FILL), turn_rows(turn(wind, FILL + CHUNK), -1))
        u = jnp.where(lane < FILL + 2 * CHUNK, u, turn(height, FILL + 2 * CHUNK))
        u = jnp.where(lane < FILL + 3 * CHUNK, u, turn_rows(turn(height, FILL + 3 * CHUNK), -1))
        left = [u, wind, height]
        g = thin[...]
        right = [turn(g, -3 * q) for q in range(3)]
        fr = jnp.where(lane < 64, turn(g, -9), turn(wind, LANES - FILL + 1))
        he = jnp.where(lane < 64, turn(g, -11), turn(wind, LANES - FILL))
        got = depart(own, left, right, depth, interp_weights(mine[3]))
        past = depart_beside(own, left, right, depth, interp_weights(fr))
        for q in range(3):
            stores.append((side, ext.at[q, 0], jnp.where(inside[side], got[q], 0.0)))
            stores.append((side, ext.at[q, 1], jnp.where(inside[side], past[q], 0.0)))
        stores.append((side, hel.at[0], mine[4]))
        stores.append((side, hel.at[1], he))
    for side, ref, value in stores:
        at = BAND - 2 if side == 0 else BAND + clat
        for k in range(lev):
            ref[k, at:at + 2, :] = value[2 * k:2 * k + 2]


def solve(lev, clat, inside, helm, ext, hel, rhs_s, p1_s, pressure):
    tall = clat + BAND
    row = lax.broadcasted_iota(jnp.int32, (lev, tall, LANES), 1)
    outside = ((row == 0) & jnp.logical_not(inside[0])) | ((row == clat + 1) & jnp.logical_not(inside[1]))
    first = BAND - 1
    flat = lambda x: x.reshape(-1, LANES)
    mid, up, down = pl.ds(first, tall), pl.ds(first - 1, tall), pl.ds(first + 1, tall)
    u_all = beside_pair(flat(ext[0, 0, :, mid, :]), flat(ext[0, 1, :, mid, :]))
    phi = [flat(ext[2, h, :, mid, :]) for h in range(2)]
    phi_all = beside_pair(*phi)
    p1, rhs = [], []
    for h in range(2):
        div = 0.5 * (u_all[h][0] - u_all[h][1] + flat(ext[1, h, :, down, :]) - flat(ext[1, h, :, up, :]))
        rhs.append(phi[h] - 0.5 * div)
        around = phi_all[h][0] + phi_all[h][1] + flat(ext[2, h, :, down, :]) + flat(ext[2, h, :, up, :])
        p1.append((rhs[h] + around) / (4.0 + flat(hel[h, :, mid, :])))
    for h in range(2):
        p1_s[h] = jnp.where(outside, 0.0, p1[h].reshape(lev, tall, LANES))
    rhs_s[...] = rhs[0].reshape(lev, tall, LANES)
    mid = pl.ds(1, clat)
    east, west = beside_pair(flat(p1_s[0, :, mid, :]), flat(p1_s[1, :, mid, :]))[0]
    around = east + west + flat(p1_s[0, :, pl.ds(2, clat), :]) + flat(p1_s[0, :, pl.ds(0, clat), :])
    pressure[...] = ((flat(rhs_s[:, mid, :]) + around) / (4.0 + flat(helm[...]))).reshape(lev, clat, LANES)


def store(departed, pressure, departed_o, pressure_o, sem):
    copies = [pltpu.make_async_copy(departed, departed_o, sem.at[0]), pltpu.make_async_copy(pressure, pressure_o, sem.at[1])]
    for c in copies:
        c.start()
    for c in copies:
        c.wait()


def local(fields, depth, frac, helm):
    lev, clat, clon = fields.shape[1:]
    hbm = pl.BlockSpec(memory_space=pltpu.HBM)
    vmem = pl.BlockSpec(memory_space=pltpu.VMEM)
    sent = [(5, lev + REST[-1][0] + 1, BAND, clon), (lev, BAND, clon), (6, 2 * lev, clon), (6, 2 * lev, clon),
            (2, 2 * lev, clon), (2, 2 * lev, clon), (2 * lev, clon), (2 * lev, clon)]
    tall = clat + 2 * BAND
    departed, pressure = pl.pallas_call(
        functools.partial(whole_step, lev, clat),
        out_shape=[pltpu.VMEM(fields.shape, F32), pltpu.VMEM(frac.shape, F32)],
        in_specs=[hbm] * 4,
        out_specs=[vmem, vmem],
        scratch_shapes=[
            pltpu.SMEM(depth.shape, jnp.int32),
            pltpu.VMEM(fields.shape, F32), pltpu.VMEM(frac.shape, F32), pltpu.VMEM(helm.shape, F32),
            *[pltpu.VMEM(t, F32) for t in sent],
            *[pltpu.VMEM(t, F32) for t in sent],
            pltpu.VMEM((3, 2, lev, tall, clon), F32),
            pltpu.VMEM((2, lev, tall, clon), F32),
            pltpu.VMEM((lev, clat + BAND, clon), F32),
            pltpu.VMEM((2, lev, clat + BAND, clon), F32),
            pltpu.VMEM((4, *frac.shape), F32),
            pltpu.VMEM((4, *frac.shape), F32),
            pltpu.VMEM(frac.shape, F32),
            pltpu.SemaphoreType.DMA((8,)),
            pltpu.SemaphoreType.DMA((12,)),
            pltpu.SemaphoreType.DMA((12,)),
            pltpu.SemaphoreType.REGULAR,
        ],
        compiler_params=pltpu.CompilerParams(collective_id=0, has_side_effects=True, vmem_limit_bytes=24 << 20),
        name="step",
    )(*[pltpu.with_memory_space_constraint(x, pltpu.HBM) for x in (depth, fields, frac, helm)])
    return pl.pallas_call(
        store,
        out_shape=[jax.ShapeDtypeStruct(fields.shape, F32), jax.ShapeDtypeStruct(frac.shape, F32)],
        in_specs=[vmem, vmem],
        out_specs=[hbm, hbm],
        scratch_shapes=[pltpu.SemaphoreType.DMA((2,))],
        compiler_params=pltpu.CompilerParams(vmem_limit_bytes=1 << 20),
        name="store",
    )(*[pltpu.with_memory_space_constraint(x, pltpu.VMEM) for x in (departed, pressure)])


def solution(mesh):
    placed = (P(None, None, "lat", "lon"), P("lat"), P(None, "lat", "lon"), P(None, "lat", "lon"))
    return jax.shard_map(
        local,
        mesh=mesh,
        in_specs=placed,
        out_specs=(P(None, None, "lat", "lon"), P(None, "lat", "lon")),
        check_vma=False,
    )
```
